128 devices in a mesh: seq: 64 (over z, x, y_lo, core), tp: 2 (over y_hi).
Axes of the slice: x: 4, y: 4 (y_hi: 2, y_lo: 2; y = y_hi * 2 + y_lo), z: 4, core: 2. Of those that a mesh axis runs over, the one named last changes fastest.
Arguments:
- latent: bfloat16 [64, 512, 1152], P('seq', 'tp'), may hold values from -6 to 6
- probe: bfloat16 [64, 512, 1152], P('seq', 'tp'), may hold values from -6 to 6
- adjoint: bfloat16 [64, 512, 1152], P('seq', 'tp'), may hold values from -6 to 6
- spatial_qkv: bfloat16 [1152, 3, 1152], P(None, None, 'tp'), may hold values from -0.1875 to 0.1875
- spatial_proj: bfloat16 [1152, 1152], P('tp'), may hold values from -0.75 to 0.75
- temporal_qkv: bfloat16 [1152, 3, 1152], P(None, None, 'tp'), may hold values from -0.1875 to 0.1875
- temporal_proj: bfloat16 [1152, 1152], P('tp'), may hold values from -0.75 to 0.75
Outputs:
- new_latent: bfloat16 [64, 512, 1152], P('seq', 'tp')
- new_adjoint: float32 [64, 512, 1152], P('seq', 'tp')
- trace_terms: float32 [64, 512], P('seq', 'tp')
The draws below stay inside these ranges and needn't reach their ends.
All inputs are finite; a program needn't handle non-finite values.
Results may differ from the reference program's by a relative error of at most 0.025.
Values may be sent and summed in bfloat16 or wider, within the bound.
A program may use at most 192 MiB of HBM per device.

```python
import jax
import jax.numpy as jnp
from jax import lax

D = 1152
HEAD = 72
S = 512
FRAMES = 64


def level_of(rng, shape, shards, least, top_value):
    level, own = 1.0, jax.random.fold_in(rng, 6)
    for dim, parts in shards:
        steps = jnp.exp(jax.random.uniform(jax.random.fold_in(own, dim), (parts,), jnp.float32, least / len(shards), top_value / len(shards)))
        level = level * jnp.repeat(steps, shape[dim] // parts).reshape([-1 if axis == dim else 1 for axis in range(len(shape))])
    return level


def bell_draw(rng, dims, deviation, limit, cuts=(), kind=jnp.bfloat16):
    values = deviation * jax.random.normal(rng, dims, jnp.float32)
    if cuts:
        values = values * level_of(rng, dims, cuts, -0.22, 0.18)
    return jnp.clip(values, -limit, limit).astype(kind)


def setup_inputs(seed: int = 0) -> dict:
    keys = jax.random.split(jax.random.key(seed), 8)
    latent = bell_draw(keys[0], (FRAMES, S, D), 1.0, 6.0, ((0, 64), (1, 2)))
    probe = bell_draw(keys[1], (FRAMES, S, D), 1.0, 6.0, ((0, 64), (1, 2)))
    adjoint = bell_draw(keys[2], (FRAMES, S, D), 1.0, 6.0, ((0, 64), (1, 2)))
    spatial_qkv = bell_draw(keys[3], (D, 3, D), D ** -0.5, 0.1875, ((2, 2),))
    spatial_proj = bell_draw(keys[4], (D, D), 64 ** -0.5, 0.75, ((0, 2),))
    temporal_qkv = bell_draw(keys[5], (D, 3, D), D ** -0.5, 0.1875, ((2, 2),))
    temporal_proj = bell_draw(keys[6], (D, D), 64 ** -0.5, 0.75, ((0, 2),))
    return {"latent": latent, "probe": probe, "adjoint": adjoint, "spatial_qkv": spatial_qkv, "spatial_proj": spatial_proj, "temporal_qkv": temporal_qkv, "temporal_proj": temporal_proj}


epsilon = 1e-06
step_size = 0.5

def contract(form, left, right):
    return jnp.einsum(form, left.astype(jnp.float32), right.astype(jnp.float32))

def norm_stats(values):
    widened = values.astype(jnp.float32)
    centred = widened - lax.optimization_barrier(jnp.mean(widened, axis=-1, keepdims=True))
    inverse = lax.rsqrt(lax.optimization_barrier(jnp.mean(centred * centred, axis=-1, keepdims=True)) + epsilon)
    return (centred * inverse, inverse)

def norm_tangent(normed, inverse, tangent):
    widened = tangent.astype(jnp.float32)
    centred = widened - lax.optimization_barrier(jnp.mean(widened, axis=-1, keepdims=True))
    return inverse * (centred - normed * lax.optimization_barrier(jnp.mean(normed * centred, axis=-1, keepdims=True)))

def norm_back(normed, inverse, gradient):
    return inverse * (gradient - lax.optimization_barrier(jnp.mean(gradient, axis=-1, keepdims=True)) - normed * lax.optimization_barrier(jnp.mean(normed * gradient, axis=-1, keepdims=True)))

def project(hidden, w_qkv):
    lead_dim, second = (hidden.shape[0], hidden.shape[1])
    head_count = w_qkv.shape[2] // HEAD
    projected = contract('abd,dcn->cabn', hidden, w_qkv).astype(jnp.bfloat16)
    return projected.reshape(3, lead_dim, second, head_count, HEAD)

def attend(projected, rows_spec, keys_spec):
    scores = contract(rows_spec + ',' + keys_spec + '->ghlm', projected[0], projected[1]) * HEAD ** (-0.5)
    attention = jax.nn.softmax(scores, axis=-1)
    weights = attention.astype(jnp.bfloat16)
    mixed_rows = contract('ghlm,' + keys_spec + '->' + rows_spec, weights, projected[2]).astype(jnp.bfloat16)
    return (attention, weights, mixed_rows)

def attend_tangent(projected, tangents, attention, weights, rows_spec, keys_spec):
    to_scores = rows_spec + ',' + keys_spec + '->ghlm'
    to_rows = 'ghlm,' + keys_spec + '->' + rows_spec
    score_tangent = (contract(to_scores, tangents[0], projected[1]) + contract(to_scores, projected[0], tangents[1])) * HEAD ** (-0.5)
    prob_tangent = attention * (score_tangent - lax.optimization_barrier(jnp.sum(attention * score_tangent, axis=-1, keepdims=True)))
    mixed_tangent = contract(to_rows, prob_tangent.astype(jnp.bfloat16), projected[2]) + contract(to_rows, weights, tangents[2])
    return mixed_tangent.astype(jnp.bfloat16)

def attend_back(projected, attention, weights, grad_mixed, rows_spec, keys_spec):
    to_scores = rows_spec + ',' + keys_spec + '->ghlm'
    to_rows = 'ghlm,' + keys_spec + '->' + rows_spec
    to_keys = 'ghlm,' + rows_spec + '->' + keys_spec
    grad_weights = contract(to_scores, grad_mixed, projected[2])
    grad_value = contract(to_keys, weights, grad_mixed).astype(jnp.bfloat16)
    grad_scores = attention * (grad_weights - lax.optimization_barrier(jnp.sum(attention * grad_weights, axis=-1, keepdims=True))) * HEAD ** (-0.5)
    grad_scores = grad_scores.astype(jnp.bfloat16)
    grad_query = contract(to_rows, grad_scores, projected[1]).astype(jnp.bfloat16)
    grad_key = contract(to_keys, grad_scores, projected[0]).astype(jnp.bfloat16)
    return jnp.stack([grad_query, grad_key, grad_value])

def out_proj(mixed_rows, w_proj):
    flat_rows = mixed_rows.reshape(mixed_rows.shape[0], mixed_rows.shape[1], -1)
    return contract('abn,nd->abd', flat_rows, w_proj)

def block_primal(values, w_qkv, w_proj, rows_spec, keys_spec):
    normed, inverse = norm_stats(values)
    projected = project(normed.astype(jnp.bfloat16), w_qkv)
    attention, weights, mixed_rows = attend(projected, rows_spec, keys_spec)
    return (out_proj(mixed_rows, w_proj), (normed, inverse, projected, attention, weights))

def block_tangent(stored, tangent, w_qkv, w_proj, rows_spec, keys_spec):
    normed, inverse, projected, attention, weights = stored
    hidden_tangent = norm_tangent(normed, inverse, tangent).astype(jnp.bfloat16)
    tangents = project(hidden_tangent, w_qkv)
    return out_proj(attend_tangent(projected, tangents, attention, weights, rows_spec, keys_spec), w_proj)

def block_back(stored, gradient, w_qkv, w_proj, rows_spec, keys_spec):
    normed, inverse, projected, attention, weights = stored
    grad_mixed = contract('abd,nd->abn', gradient, w_proj).astype(jnp.bfloat16).reshape(projected.shape[1:])
    grad_stack = attend_back(projected, attention, weights, grad_mixed, rows_spec, keys_spec)
    flat_grads = grad_stack.reshape(3, grad_stack.shape[1], grad_stack.shape[2], -1)
    return contract('cabn,dcn->abd', flat_grads, w_qkv)

def reference(latent, probe, adjoint, spatial_qkv, spatial_proj, temporal_qkv, temporal_proj):

    def spatial_forward(entries):
        branch, stored = block_primal(entries[0][None], spatial_qkv, spatial_proj, 'glhe', 'gmhe')
        dbranch = block_tangent(stored, entries[1][None], spatial_qkv, spatial_proj, 'glhe', 'gmhe')
        return (branch[0], dbranch[0])
    branch_one, dbranch_one = lax.map(spatial_forward, (latent, probe))
    inner_rows = (latent.astype(jnp.float32) + branch_one).astype(jnp.bfloat16)
    inner_tangent = (probe.astype(jnp.float32) + dbranch_one).astype(jnp.bfloat16)

    def to_blocks(values):
        return jnp.moveaxis(values.reshape(FRAMES, S // 8, 8, D), 1, 0)

    def from_blocks(values):
        return jnp.moveaxis(values, 0, 1).reshape(FRAMES, S, D)

    def temporal_all(entries):
        branch, stored = block_primal(entries[0], temporal_qkv, temporal_proj, 'lghe', 'mghe')
        dbranch = block_tangent(stored, entries[1], temporal_qkv, temporal_proj, 'lghe', 'mghe')
        grad_hidden = block_back(stored, entries[2], temporal_qkv, temporal_proj, 'lghe', 'mghe')
        grad_rows = norm_back(stored[0], stored[1], grad_hidden)
        return (branch.astype(jnp.bfloat16), dbranch.astype(jnp.bfloat16), grad_rows.astype(jnp.bfloat16))
    results = lax.map(temporal_all, (to_blocks(inner_rows), to_blocks(inner_tangent), to_blocks(adjoint)))
    branch_two = from_blocks(results[0])
    dbranch_two = from_blocks(results[1])
    grad_two = from_blocks(results[2])
    grads_one = (adjoint.astype(jnp.float32) + grad_two.astype(jnp.float32)).astype(jnp.bfloat16)

    def spatial_backward(entries):
        branch, stored = block_primal(entries[0][None], spatial_qkv, spatial_proj, 'glhe', 'gmhe')
        grad_hidden = block_back(stored, entries[1][None], spatial_qkv, spatial_proj, 'glhe', 'gmhe')
        return norm_back(stored[0], stored[1], grad_hidden)[0]
    grad_one = lax.map(spatial_backward, (latent, grads_one))
    velocity = branch_one + branch_two.astype(jnp.float32)
    new_latent = (latent.astype(jnp.float32) + step_size * velocity).astype(jnp.bfloat16)
    trace_terms = lax.optimization_barrier(jnp.mean(probe.astype(jnp.float32) * (dbranch_one + dbranch_two.astype(jnp.float32)), axis=-1))
    new_adjoint = adjoint.astype(jnp.float32) - step_size * (grad_one + grad_two.astype(jnp.float32))
    return (new_latent, new_adjoint, trace_terms)
```

```python
import jax
import jax.numpy as jnp
from jax import lax
from jax.experimental import pallas as pl
from jax.experimental.pallas import tpu as pltpu
from jax.sharding import PartitionSpec as P

MESH = pl.DeviceIdType.MESH
BF = jnp.bfloat16
F32 = jnp.float32

epsilon = 1e-06
HEAD = 72
D = 1152
ROWS = 256
HALF = 576
PAD = 640
WIN = 256
GROUP = 64
SPAN = 4
SCALE = HEAD ** (-0.5)
EXP2 = SCALE * 1.4426950408889634


def nt(a, b):
    return lax.dot_general(a, b, (((1,), (1,)), ((), ())), preferred_element_type=F32)


def nn(a, b):
    return lax.dot_general(a, b, (((1,), (0,)), ((), ())), preferred_element_type=F32)


def tn(a, b):
    return lax.dot_general(a, b, (((0,), (0,)), ((), ())), preferred_element_type=F32)


def mean(v):
    return jnp.sum(v, axis=-1, keepdims=True) * (1.0 / D)


def norm_stats(x):
    centred = x - mean(x)
    inverse = lax.rsqrt(mean(centred * centred) + epsilon)
    return centred * inverse, inverse


def norm_tangent(normed, inverse, t):
    centred = t - mean(t)
    return inverse * (centred - normed * mean(normed * centred))


def norm_back(normed, inverse, g):
    return inverse * (g - mean(g) - normed * mean(normed * g))


def weight(ref, kind):
    return ref[kind].reshape(HALF, D)


def head_window(h):
    block = jnp.minimum(lax.div(h * 9, 16), 3)
    base = pl.multiple_of(block * 128, 128)
    lane = lax.broadcasted_iota(jnp.int32, (1, WIN), 1) + block * 128
    return pl.ds(base, WIN), (lane >= h * HEAD) & (lane < h * HEAD + HEAD)


def keep(mask, v):
    return jnp.where(mask, v, jnp.zeros_like(v))


def rank():
    s, t = lax.axis_index("seq"), lax.axis_index("tp")
    return s, t, lax.rem(s, 2)


def kernel(
    latent, probe, adjoint, wsq, wsp, wtq, wtp,
    o_latent, o_adjoint, o_trace,
    ws_own, ws_oth, wt_own, wt_oth,
    own_lat, own_prb, own_adj, x_lat, x_prb,
    hid, sq, sk, sv, sdq, sdk, sdv, probs,
    tq, tk, tv, tdq, tdk, tdv, tprobs,
    mix, gq, gk, gv, gsib_out, gsib_in, gh,
    m_inner, m_tan, m_adj, r_inner, r_tan, r_adj,
    m_g, m_u, m_d, r_g, r_u, r_d,
    v_out, v_in, tr_out, tr_in,
    l_sem, w_sem, swap_s, swap_r, sib_s, sib_r,
    gat_s, gat_r, fw_s, fw_r, a2a_s, a2a_r, gs_s, gs_r, end_s, end_r,
):
    s, t, c = rank()
    zx = lax.div(s, 4)
    z, x = lax.div(zx, 4), lax.rem(zx, 4)
    low = lax.rem(s, 4)
    stay = c == t
    swap_dev = (s - c + t, c)
    sib_dev = (s + 1 - 2 * c, t)
    y_dev = (s + 2 - 4 * lax.rem(lax.div(s, 2), 2), 1 - t)

    def remote(src, dst, ss, rs, dev):
        return pltpu.make_async_remote_copy(
            src_ref=src, dst_ref=dst, send_sem=ss, recv_sem=rs, device_id=dev, device_id_type=MESH
        )

    local = [
        pltpu.make_async_copy(wsq, ws_own.at[pl.ds(0, 3)], w_sem.at[0]),
        pltpu.make_async_copy(wsp, ws_own.at[3], w_sem.at[1]),
        pltpu.make_async_copy(latent.at[0], own_lat, l_sem.at[0]),
        pltpu.make_async_copy(probe.at[0], own_prb, l_sem.at[1]),
        pltpu.make_async_copy(adjoint.at[0], own_adj, l_sem.at[2]),
        pltpu.make_async_copy(wtq, wt_own.at[pl.ds(0, 3)], w_sem.at[2]),
        pltpu.make_async_copy(wtp, wt_own.at[3], w_sem.at[3]),
    ]
    for copy in local:
        copy.start()
    barrier = pltpu.get_barrier_semaphore()
    me = s * 2 + t

    def greet(k, carry):
        other = lax.rem(me + k, 2 * GROUP)
        pl.semaphore_signal(
            barrier, inc=1, device_id=(lax.div(other, 2), lax.rem(other, 2)), device_id_type=MESH
        )
        return carry

    lax.fori_loop(1, 2 * GROUP, greet, 0)
    for ref in (sq, sdq, tq, tdq):
        ref[:, :, pl.ds(HALF, PAD - HALF)] = jnp.zeros((2, ROWS, PAD - HALF), BF)
    for copy in local:
        copy.wait()
    pl.semaphore_wait(barrier, 2 * GROUP - 1)

    def parts(emit):
        for core, first, size in ((0, 0, 80), (1, 80, 64)):
            @pl.when(c == core)
            def _(core=core, first=first, size=size):
                emit(core, pl.ds(first, size), size)

    def line(ref, core, i, j, rows):
        if core == 0:
            return ref.at[i, :, rows, :]
        return ref.at[:, j, rows, :]

    def hop(core, k):
        if core == 0:
            return (lax.rem(z + k, 4) * 16 + x * 4 + low, t)
        return (z * 16 + lax.rem(x + k, 4) * 4 + low, t)

    def step(core, k):
        if core == 0:
            return (z * 16 + lax.rem(x + k, 4) * 4 + low, t)
        return (lax.rem(z + k, 4) * 16 + x * 4 + low, t)

    def gather_first(n, own, oth):
        def emit(core, rows, size):
            remote(
                own.at[z, x, rows, :], oth.at[z, x, rows, :],
                gat_s.at[n, 0], gat_r.at[n, 0], y_dev,
            ).start()
        parts(emit)

    def gather_second(n, own, oth):
        def emit(core, rows, size):
            remote(
                own.at[z, x, rows, :], oth.at[z, x, rows, :],
                gat_s.at[n, 0], gat_r.at[n, 0], y_dev,
            ).wait()
            for k in range(1, 4):
                remote(
                    oth.at[z, x, rows, :], oth.at[z, x, rows, :],
                    gat_s.at[n, k], gat_r.at[n, k], step(core, k),
                ).start()
        parts(emit)

    def gather_third(n, oth):
        def emit(core, rows, size):
            for k in range(1, 4):
                remote(
                    oth.at[z, x, rows, :], oth.at[z, x, rows, :],
                    gat_s.at[n, k], gat_r.at[n, k], step(core, k),
                ).wait()
            whole = line(oth, core, z, x, rows)
            for k in range(1, 4):
                remote(
                    whole, whole, gat_s.at[n, 3 + k], gat_r.at[n, 3 + k], hop(core, k)
                ).start()
            remote(whole, whole, fw_s.at[n, 0], fw_r.at[n, 0], sib_dev).start()
        parts(emit)

    def gather_fourth(n, oth):
        def emit(core, rows, size):
            for k in (1, 3, 2):
                came = line(oth, core, lax.rem(z - k + 4, 4), lax.rem(x - k + 4, 4), rows)
                remote(
                    came, came, gat_s.at[n, 3 + k], gat_r.at[n, 3 + k], hop(core, k)
                ).wait_recv()
                remote(came, came, fw_s.at[n, k], fw_r.at[n, k], sib_dev).start()
        parts(emit)

    def gather_last(n, oth):
        def emit(core, rows, size):
            whole = line(oth, core, z, x, rows)
            other_rows = pl.ds(80, 64) if core == 0 else pl.ds(0, 80)
            theirs = line(oth, 1 - core, z, x, other_rows)
            for k in range(4):
                remote(theirs, theirs, fw_s.at[n, k], fw_r.at[n, k], sib_dev).wait_recv()
                remote(whole, whole, fw_s.at[n, k], fw_r.at[n, k], sib_dev).wait_send()
            for k in range(1, 4):
                remote(
                    whole, whole, gat_s.at[n, 3 + k], gat_r.at[n, 3 + k], hop(core, k)
                ).wait_send()
        parts(emit)

    def exchange(n, src, dst, place, device, selfless):
        def send(k, carry):
            j = lax.rem(s + k, GROUP)
            remote(src.at[j], dst.at[place], a2a_s.at[n], a2a_r.at[n], device(j)).start()
            return carry

        if selfless is None:
            pltpu.make_async_copy(src.at[s], dst.at[s], a2a_r.at[n]).start()
        else:
            @pl.when(selfless)
            def _():
                pltpu.make_async_copy(src.at[s], dst.at[s], a2a_r.at[n]).start()

            @pl.when(jnp.logical_not(selfless))
            def _():
                send(0, 0)
        lax.fori_loop(1, GROUP, send, 0)

    def received(n, dst):
        remote(dst, dst, a2a_s.at[n], a2a_r.at[n], sib_dev).wait_recv()

    def sent(n, src, selfless):
        some = src.at[pl.ds(0, GROUP - 1)]
        remote(some, some, a2a_s.at[n], a2a_r.at[n], sib_dev).wait_send()
        if selfless is not None:
            @pl.when(jnp.logical_not(selfless))
            def _():
                one = src.at[0]
                remote(one, one, a2a_s.at[n], a2a_r.at[n], sib_dev).wait_send()

    def to_sibling(half, n, ref):
        return remote(
            ref.at[half, pl.ds(0, ROWS)], ref.at[half, pl.ds(ROWS, ROWS)],
            sib_s.at[half, n], sib_r.at[half, n], sib_dev,
        )

    frame = s - c + t

    gather_first(0, ws_own, ws_oth)

    @pl.when(jnp.logical_not(stay))
    def _():
        remote(own_lat, x_lat, swap_s.at[0], swap_r.at[0], swap_dev).start()
        remote(own_prb, x_prb, swap_s.at[1], swap_r.at[1], swap_dev).start()

    m_adj[...] = own_adj[...].reshape(GROUP, SPAN, D)
    gather_second(0, ws_own, ws_oth)

    def arrive(n, own, ref):
        @pl.when(stay)
        def _():
            ref[...] = own[...]

        @pl.when(jnp.logical_not(stay))
        def _():
            remote(own, ref, swap_s.at[n], swap_r.at[n], swap_dev).wait()

    arrive(0, own_lat, x_lat)
    hid[0] = norm_stats(x_lat[...].astype(F32))[0].astype(BF)

    def project(half, w, slot, q_ref, k_ref, v_ref, q_scale, exchange_rows):
        hidden = hid[slot]
        lanes = pl.ds(0, HALF)
        rows = pl.ds(0, ROWS)
        key = nt(hidden, weight(w, 1))
        k_ref[half, rows, lanes] = key.astype(BF)
        if exchange_rows is not None:
            to_sibling(half, exchange_rows, k_ref).start()
        v_ref[half, rows, lanes] = nt(hidden, weight(w, 2)).astype(BF)
        if exchange_rows is not None:
            to_sibling(half, exchange_rows + 1, v_ref).start()
        q_ref[half, rows, lanes] = nt(hidden, weight(w, 0)).astype(BF)

    def spatial_heads(half):
        mix[half] = jnp.zeros((ROWS, PAD), F32)

        def body(h, carry):
            win, mask = head_window(h)
            k = keep(mask, sk[half, :, win])
            scores = nt(sq[half, :, win], k)
            e = jnp.exp2((scores - jnp.max(scores, axis=-1, keepdims=True)) * EXP2)
            p = e * (1.0 / jnp.sum(e, axis=-1, keepdims=True))
            w = p.astype(BF)
            probs[half * 8 + h] = w
            mix[half, :, win] += nn(w, keep(mask, sv[half, :, win]))
            return carry

        lax.fori_loop(0, 8, body, 0)

    def tangent_heads(half, q_ref, k_ref, v_ref, dq_ref, dk_ref, dv_ref, p_ref):
        mix[half] = jnp.zeros((ROWS, PAD), F32)

        def body(h, carry):
            win, mask = head_window(h)
            k = keep(mask, k_ref[half, :, win])
            dk = keep(mask, dk_ref[half, :, win])
            ds = nt(dq_ref[half, :, win], k) + nt(q_ref[half, :, win], dk)
            w = p_ref[half * 8 + h]
            p = w.astype(F32)
            pd = p * (ds * SCALE)
            dp = (pd - p * jnp.sum(pd, axis=-1, keepdims=True)).astype(BF)
            out = nn(dp, keep(mask, v_ref[half, :, win]))
            out += nn(w, keep(mask, dv_ref[half, :, win]))
            mix[half, :, win] += out
            return carry

        lax.fori_loop(0, 8, body, 0)

    def out_proj(w_own, w_oth):
        lanes = pl.ds(0, HALF)
        first = nn(mix[0, :, lanes].astype(BF), weight(w_own, 3))
        return first + nn(mix[1, :, lanes].astype(BF), weight(w_oth, 3))

    project(0, ws_own, 0, sq, sk, sv, None, 0)
    gather_third(0, ws_oth)
    for n, ref in ((0, sk), (1, sv)):
        to_sibling(0, n, ref).wait()
    spatial_heads(0)
    gather_fourth(0, ws_oth)
    gather_last(0, ws_oth)
    project(1, ws_oth, 0, sq, sk, sv, None, 0)
    for n, ref in ((0, sk), (1, sv)):
        to_sibling(1, n, ref).wait()
    spatial_heads(1)
    inner = (x_lat[...].astype(F32) + out_proj(ws_own, ws_oth)).astype(BF)
    m_inner[...] = inner.reshape(GROUP, SPAN, D)
    exchange(0, m_inner, r_inner, frame, lambda j: (j, c), stay)
    exchange(1, m_adj, r_adj, s, lambda j: (j, t), None)
    gather_first(1, wt_own, wt_oth)

    arrive(1, own_prb, x_prb)
    normed, inverse = norm_stats(x_lat[...].astype(F32))
    hid[1] = norm_tangent(normed, inverse, x_prb[...].astype(F32)).astype(BF)
    project(0, ws_own, 1, sdq, sdk, sdv, None, 2)
    project(1, ws_oth, 1, sdq, sdk, sdv, None, 2)
    gather_second(1, wt_own, wt_oth)
    for half in range(2):
        for n, ref in ((2, sdk), (3, sdv)):
            to_sibling(half, n, ref).wait()
        tangent_heads(half, sq, sk, sv, sdq, sdk, sdv, probs)
    gather_third(1, wt_oth)
    moved = out_proj(ws_own, ws_oth)
    tangent = x_prb[...].astype(F32)
    tr_out[...] = jnp.broadcast_to(mean(tangent * moved), (ROWS, 128))
    m_tan[...] = (tangent + moved).astype(BF).reshape(GROUP, SPAN, D)
    exchange(2, m_tan, r_tan, frame, lambda j: (j, c), stay)

    row = lax.broadcasted_iota(jnp.int32, (ROWS, ROWS), 0)
    col = lax.broadcasted_iota(jnp.int32, (ROWS, ROWS), 1)
    same = lax.rem(row, SPAN) == lax.rem(col, SPAN)

    received(0, r_inner)
    x_inner = r_inner[...].reshape(ROWS, D).astype(F32)
    hid[0] = norm_stats(x_inner)[0].astype(BF)
    received(1, r_adj)

    def back_lanes(half, w, g):
        gm = nt(g, weight(w, 3)).astype(BF)
        sdq[half, :, pl.ds(0, HALF)] = gm

    def temporal_heads(half):
        mix[half] = jnp.zeros((ROWS, PAD), F32)
        gq[...] = jnp.zeros(gq.shape, F32)
        gk[...] = jnp.zeros(gk.shape, F32)
        gv[...] = jnp.zeros(gv.shape, F32)

        def body(h, carry):
            win, mask = head_window(h)
            q = tq[half, :, win]
            k = keep(mask, tk[half, :, win])
            v = keep(mask, tv[half, :, win])
            g = sdq[half, :, win]
            scores = jnp.where(same, nt(q, k), -1e30)
            e = jnp.exp2((scores - jnp.max(scores, axis=-1, keepdims=True)) * EXP2)
            p = e * (1.0 / jnp.sum(e, axis=-1, keepdims=True))
            w = p.astype(BF)
            tprobs[half * 8 + h] = w
            mix[half, :, win] += nn(w, v)
            gw = nt(g, v)
            pg = p * (gw * SCALE)
            gs = (pg - p * jnp.sum(pg, axis=-1, keepdims=True)).astype(BF)
            gq[:, win] += nn(gs, k)
            gk[pl.ds(0, ROWS), win] += tn(gs, keep(mask, q))
            gv[pl.ds(0, ROWS), win] += tn(w, keep(mask, g))
            return carry

        lax.fori_loop(0, 8, body, 0)

    def hidden_back(w):
        lanes = pl.ds(0, HALF)
        rows = pl.ds(0, ROWS)
        out = nn(gq[:, lanes].astype(BF), weight(w, 0))
        out += nn(gk[rows, lanes].astype(BF), weight(w, 1))
        return out + nn(gv[rows, lanes].astype(BF), weight(w, 2))

    g_two = r_adj[...].reshape(ROWS, D)
    project(0, wt_own, 0, tq, tk, tv, None, None)
    back_lanes(0, wt_own, g_two)
    temporal_heads(0)
    gh[...] = hidden_back(wt_own)
    gather_fourth(1, wt_oth)
    gather_last(1, wt_oth)
    project(1, wt_oth, 0, tq, tk, tv, None, None)
    back_lanes(1, wt_oth, r_adj[...].reshape(ROWS, D))
    temporal_heads(1)
    g_hidden = gh[...] + hidden_back(wt_oth)
    normed, inverse = norm_stats(r_inner[...].reshape(ROWS, D).astype(F32))
    grad_two = norm_back(normed, inverse, g_hidden).astype(BF).astype(F32)
    grads_one = (r_adj[...].reshape(ROWS, D).astype(F32) + grad_two).astype(BF)
    m_g[...] = grads_one.reshape(GROUP, SPAN, D)
    exchange(
        3, m_g, r_g, s, lambda f: (lax.div(f, 2) * 2 + t, lax.rem(f, 2)), stay
    )
    reached = r_inner[...].reshape(ROWS, D).astype(F32) + out_proj(wt_own, wt_oth)
    m_u[...] = reached.astype(BF).reshape(GROUP, SPAN, D)
    exchange(4, m_u, r_u, s, lambda f: (f, t), None)

    received(2, r_tan)
    normed, inverse = norm_stats(r_inner[...].reshape(ROWS, D).astype(F32))
    hid[1] = norm_tangent(normed, inverse, r_tan[...].reshape(ROWS, D).astype(F32)).astype(BF)
    project(0, wt_own, 1, tdq, tdk, tdv, None, None)
    project(1, wt_oth, 1, tdq, tdk, tdv, None, None)
    for half in range(2):
        tangent_heads(half, tq, tk, tv, tdq, tdk, tdv, tprobs)
    m_d[...] = out_proj(wt_own, wt_oth).astype(BF).reshape(GROUP, SPAN, D)
    exchange(5, m_d, r_d, s, lambda f: (f, t), None)

    received(3, r_g)

    def spatial_back(half):
        gq[...] = jnp.zeros(gq.shape, F32)
        gk[...] = jnp.zeros(gk.shape, F32)
        gv[...] = jnp.zeros(gv.shape, F32)

        def body(h, carry):
            win, mask = head_window(h)
            g = sdq[half, :, win]
            w = probs[half * 8 + h]
            p = w.astype(F32)
            gw = nt(g, keep(mask, sv[half, :, win]))
            pg = p * (gw * SCALE)
            gs = (pg - p * jnp.sum(pg, axis=-1, keepdims=True)).astype(BF)
            gq[:, win] += nn(gs, keep(mask, sk[half, :, win]))
            gk[:, win] += tn(gs, keep(mask, sq[half, :, win]))
            gv[:, win] += tn(w, keep(mask, g))
            return carry

        lax.fori_loop(0, 8, body, 0)

    def key_back(half):
        return remote(
            gsib_out.at[half], gsib_in.at[half], gs_s.at[half], gs_r.at[half], sib_dev
        )

    for half, w in ((0, ws_own), (1, ws_oth)):
        back_lanes(half, w, r_g[...].reshape(ROWS, D))
        spatial_back(half)
        gsib_out[half, 0] = gk[pl.ds(ROWS, ROWS), :].astype(BF)
        gsib_out[half, 1] = gv[pl.ds(ROWS, ROWS), :].astype(BF)
        key_back(half).start()
        lanes = pl.ds(0, HALF)
        part = nn(gq[:, lanes].astype(BF), weight(w, 0))
        if half == 0:
            gh[...] = part
        else:
            gh[...] += part
        key_back(half).wait()
        rows = pl.ds(0, ROWS)
        key = gk[rows, lanes] + gsib_in[half, 0, :, lanes].astype(F32)
        value = gv[rows, lanes] + gsib_in[half, 1, :, lanes].astype(F32)
        part = nn(key.astype(BF), weight(w, 1)) + nn(value.astype(BF), weight(w, 2))
        gh[...] += part
    normed, inverse = norm_stats(x_lat[...].astype(F32))
    grad_one = norm_back(normed, inverse, gh[...])
    v_out[...] = (grad_one + r_g[...].reshape(ROWS, D).astype(F32)).astype(BF)

    @pl.when(jnp.logical_not(stay))
    def _():
        remote(v_out, v_in, end_s.at[0], end_r.at[0], swap_dev).start()
        remote(tr_out, tr_in, end_s.at[1], end_r.at[1], swap_dev).start()

    @pl.when(stay)
    def _():
        v_in[...] = v_out[...]
        tr_in[...] = tr_out[...]

    received(4, r_u)
    o_latent[...] = (
        0.5 * (own_lat[...].astype(F32) + r_u[...].reshape(ROWS, D).astype(F32))
    ).astype(BF)
    received(5, r_d)
    extra = mean(own_prb[...].astype(F32) * r_d[...].reshape(ROWS, D).astype(F32))
    for n, ref, selfless in (
        (0, m_inner, stay), (1, m_adj, None), (2, m_tan, stay),
        (3, m_g, stay), (4, m_u, None), (5, m_d, None),
    ):
        sent(n, ref, selfless)

    @pl.when(jnp.logical_not(stay))
    def _():
        remote(v_out, v_in, end_s.at[0], end_r.at[0], swap_dev).wait()
        remote(tr_out, tr_in, end_s.at[1], end_r.at[1], swap_dev).wait()

    o_trace[...] = tr_in[...] + extra
    o_adjoint[...] = 1.5 * own_adj[...].astype(F32) - 0.5 * v_in[...].astype(F32)


def local(latent, probe, adjoint, spatial_qkv, spatial_proj, temporal_qkv, temporal_proj):
    def qkv(w):
        return jnp.transpose(w, (1, 2, 0)).reshape(3, 4, 144, D)

    def proj(w):
        return w.reshape(4, 144, D)

    dma = pltpu.SemaphoreType.DMA
    rows = pltpu.VMEM((ROWS, D), BF)
    weights = pltpu.VMEM((4, 4, 144, D), BF)
    one = pltpu.VMEM((2, ROWS, PAD), BF)
    two = pltpu.VMEM((2, 2 * ROWS, PAD), BF)
    message = pltpu.VMEM((GROUP, SPAN, D), BF)
    scratch = (
        [weights] * 4
        + [rows] * 5
        + [pltpu.VMEM((2, ROWS, D), BF)]
        + [one, two, two, one, two, two]
        + [pltpu.VMEM((16, ROWS, 2 * ROWS), BF)]
        + [one] * 6
        + [pltpu.VMEM((16, ROWS, ROWS), BF)]
        + [pltpu.VMEM((2, ROWS, PAD), F32), pltpu.VMEM((ROWS, PAD), F32)]
        + [pltpu.VMEM((2 * ROWS, PAD), F32)] * 2
        + [pltpu.VMEM((2, 2, ROWS, PAD), BF)] * 2
        + [pltpu.VMEM((ROWS, D), F32)]
        + [message] * 12
        + [rows] * 2
        + [pltpu.VMEM((ROWS, 128), F32)] * 2
        + [dma((3,)), dma((4,)), dma((2,)), dma((2,)), dma((2, 4)), dma((2, 4))]
        + [dma((2, 7)), dma((2, 7)), dma((2, 4)), dma((2, 4))]
        + [dma((6,)), dma((6,)), dma((2,)), dma((2,)), dma((2,)), dma((2,))]
    )
    new_latent, new_adjoint, trace = pl.pallas_call(
        kernel,
        out_shape=(
            jax.ShapeDtypeStruct((ROWS, D), BF),
            jax.ShapeDtypeStruct((ROWS, D), F32),
            jax.ShapeDtypeStruct((ROWS, 128), F32),
        ),
        in_specs=[pl.BlockSpec(memory_space=pl.ANY)] * 7,
        out_specs=[pl.BlockSpec(memory_space=pltpu.VMEM)] * 3,
        scratch_shapes=scratch,
        compiler_params=pltpu.CompilerParams(
            collective_id=0, has_side_effects=True, vmem_limit_bytes=63 << 20
        ),
    )(
        latent, probe, adjoint,
        qkv(spatial_qkv), proj(spatial_proj), qkv(temporal_qkv), proj(temporal_proj),
    )
    return new_latent[None], new_adjoint[None], trace[:, 0][None]


def solution(mesh):
    in_specs = (
        P("seq", "tp", None),
        P("seq", "tp", None),
        P("seq", "tp", None),
        P(None, None, "tp"),
        P("tp", None),
        P(None, None, "tp"),
        P("tp", None),
    )
    out_specs = (P("seq", "tp", None), P("seq", "tp", None), P("seq", "tp"))
    return jax.shard_map(local, mesh=mesh, in_specs=in_specs, out_specs=out_specs, check_vma=False)
```

```python
import jax
import jax.numpy as jnp
from jax import lax
from jax.experimental import pallas as pl
from jax.experimental.pallas import tpu as pltpu
from jax.sharding import PartitionSpec as P

MESH = pl.DeviceIdType.MESH
BF = jnp.bfloat16
F32 = jnp.float32

epsilon = 1e-06
HEAD = 72
D = 1152
ROWS = 256
HALF = 576
PAD = 640
WIN = 256
GROUP = 64
SPAN = 4
SCALE = HEAD ** (-0.5)
EXP2 = SCALE * 1.4426950408889634


def nt(a, b):
    return lax.dot_general(a, b, (((1,), (1,)), ((), ())), preferred_element_type=F32)


def nn(a, b):
    return lax.dot_general(a, b, (((1,), (0,)), ((), ())), preferred_element_type=F32)


def tn(a, b):
    return lax.dot_general(a, b, (((0,), (0,)), ((), ())), preferred_element_type=F32)


def mean(v):
    return jnp.sum(v, axis=-1, keepdims=True) * (1.0 / D)


def norm_stats(x):
    centred = x - mean(x)
    inverse = lax.rsqrt(mean(centred * centred) + epsilon)
    return centred * inverse, inverse


def norm_tangent(normed, inverse, t):
    centred = t - mean(t)
    return inverse * (centred - normed * mean(normed * centred))


def norm_back(normed, inverse, g):
    return inverse * (g - mean(g) - normed * mean(normed * g))


def weight(ref, kind):
    return ref[kind].reshape(HALF, D)


def head_window(h):
    block = jnp.minimum(lax.div(h * 9, 16), 3)
    base = pl.multiple_of(block * 128, 128)
    lane = lax.broadcasted_iota(jnp.int32, (1, WIN), 1) + block * 128
    return pl.ds(base, WIN), (lane >= h * HEAD) & (lane < h * HEAD + HEAD)


def keep(mask, v):
    return jnp.where(mask, v, jnp.zeros_like(v))


def rank():
    s, t = lax.axis_index("seq"), lax.axis_index("tp")
    return s, t, lax.rem(s, 2)


def kernel(
    latent, probe, adjoint, wsq, wsp, wtq, wtp,
    o_reached, o_grads, o_trace,
    ws_own, ws_oth, wt_own, wt_oth,
    own_lat, own_prb, own_adj, x_lat, x_prb,
    hid, sq, sk, sv, sdq, sdk, sdv, probs,
    tq, tk, tv, tprobs,
    mix, dmix, gq, gk, gv, gsib_out, gsib_in, gh,
    m_inner, m_tan, m_adj, r_inner, r_tan, r_adj,
    m_g, m_u, m_d, r_g, r_u, r_d,
    v_out, v_in, tr_out, tr_in,
    l_sem, w_sem, swap_s, swap_r, sib_s, sib_r,
    gat_s, gat_r, fw_s, fw_r, a2a_s, a2a_r, gs_s, gs_r, end_s, end_r, plane_sem, all_sem,
):
    s, t, c = rank()
    zx = lax.div(s, 4)
    z, x = lax.div(zx, 4), lax.rem(zx, 4)
    low = lax.rem(s, 4)
    stay = c == t
    swap_dev = (s - c + t, c)
    sib_dev = (s + 1 - 2 * c, t)
    y_dev = (s + 2 - 4 * lax.rem(lax.div(s, 2), 2), 1 - t)

    def remote(src, dst, ss, rs, dev):
        return pltpu.make_async_remote_copy(
            src_ref=src, dst_ref=dst, send_sem=ss, recv_sem=rs, device_id=dev, device_id_type=MESH
        )

    local = [
        pltpu.make_async_copy(wsq, ws_own.at[pl.ds(0, 3)], w_sem.at[0]),
        pltpu.make_async_copy(wsp, ws_own.at[3], w_sem.at[1]),
        pltpu.make_async_copy(latent.at[0], own_lat, l_sem.at[0]),
        pltpu.make_async_copy(probe.at[0], own_prb, l_sem.at[1]),
        pltpu.make_async_copy(adjoint.at[0], own_adj, l_sem.at[2]),
        pltpu.make_async_copy(wtq, wt_own.at[pl.ds(0, 3)], w_sem.at[2]),
        pltpu.make_async_copy(wtp, wt_own.at[3], w_sem.at[3]),
    ]
    for copy in local:
        copy.start()
    y_line = [
        (zx * 4 + lax.div(lax.rem(low * 2 + t + k, 8), 2), lax.rem(low * 2 + t + k, 2))
        for k in range(1, 8)
    ]
    x_line = [(z * 16 + lax.rem(x + k, 4) * 4 + low, t) for k in range(1, 4)]
    z_line = [(lax.rem(z + k, 4) * 16 + x * 4 + low, t) for k in range(1, 4)]

    def greet(sem, devices):
        for dev in devices:
            pl.semaphore_signal(sem, inc=1, device_id=dev, device_id_type=MESH)

    barrier = pltpu.get_barrier_semaphore()
    greet(barrier, y_line + x_line + z_line)
    for ref in (sq, sdq, tq):
        ref[:, :, pl.ds(HALF, PAD - HALF)] = jnp.zeros((2, ROWS, PAD - HALF), BF)
    for copy in local[:3]:
        copy.wait()
    pl.semaphore_wait(barrier, 13)

    def parts(emit):
        for core, first, size in ((0, 0, 80), (1, 80, 64)):
            @pl.when(c == core)
            def _(core=core, first=first, size=size):
                emit(core, pl.ds(first, size), size)

    def line(ref, core, i, j, rows, some=pl.ds(0, 4)):
        if core == 0:
            return ref.at[i, some, rows, :]
        return ref.at[some, j, rows, :]

    def hop(core, k):
        if core == 0:
            return (lax.rem(z + k, 4) * 16 + x * 4 + low, t)
        return (z * 16 + lax.rem(x + k, 4) * 4 + low, t)

    def step(core, k):
        if core == 0:
            return (z * 16 + lax.rem(x + k, 4) * 4 + low, t)
        return (lax.rem(z + k, 4) * 16 + x * 4 + low, t)

    def gather_first(n, own, oth):
        def emit(core, rows, size):
            remote(
                own.at[z, x, rows, :], oth.at[z, x, rows, :],
                gat_s.at[n, 0], gat_r.at[n, 0], y_dev,
            ).start()
        parts(emit)

    def gather_second(n, own, oth):
        def emit(core, rows, size):
            remote(
                own.at[z, x, rows, :], oth.at[z, x, rows, :],
                gat_s.at[n, 0], gat_r.at[n, 0], y_dev,
            ).wait()
            for k in range(1, 4):
                remote(
                    oth.at[z, x, rows, :], oth.at[z, x, rows, :],
                    gat_s.at[n, k], gat_r.at[n, k], step(core, k),
                ).start()
        parts(emit)

    halves = (pl.ds(0, 2), pl.ds(2, 2))

    def gather_third(n, oth):
        def emit(core, rows, size):
            for k in range(1, 4):
                remote(
                    oth.at[z, x, rows, :], oth.at[z, x, rows, :],
                    gat_s.at[n, k], gat_r.at[n, k], step(core, k),
                ).wait()
            whole = line(oth, core, z, x, rows)
            for k, m in ((1, 4), (3, 6)):
                remote(whole, whole, gat_s.at[n, m], gat_r.at[n, m], hop(core, k)).start()
            remote(whole, whole, fw_s.at[n, 0], fw_r.at[n, 0], sib_dev).start()
        parts(emit)

    def gather_fourth(n, oth):
        def emit(core, rows, size):
            for k, m, some in ((1, 4, halves[0]), (3, 6, halves[1])):
                i, j = lax.rem(z - k + 4, 4), lax.rem(x - k + 4, 4)
                came = line(oth, core, i, j, rows)
                part = line(oth, core, i, j, rows, some)
                remote(came, came, gat_s.at[n, m], gat_r.at[n, m], hop(core, k)).wait_recv()
                remote(part, part, gat_s.at[n, m + 1], gat_r.at[n, m + 1], hop(core, k)).start()
                remote(came, came, fw_s.at[n, k], fw_r.at[n, k], sib_dev).start()
        parts(emit)

    def gather_fifth(n, oth):
        def emit(core, rows, size):
            i, j = lax.rem(z + 2, 4), lax.rem(x + 2, 4)
            for k, m, some in ((1, 5, halves[0]), (3, 7, halves[1])):
                part = line(oth, core, i, j, rows, some)
                remote(part, part, gat_s.at[n, m], gat_r.at[n, m], hop(core, k)).wait_recv()
            came = line(oth, core, i, j, rows)
            remote(came, came, fw_s.at[n, 2], fw_r.at[n, 2], sib_dev).start()
        parts(emit)

    def gather_last(n, oth):
        def emit(core, rows, size):
            whole = line(oth, core, z, x, rows)
            other_rows = pl.ds(80, 64) if core == 0 else pl.ds(0, 80)
            theirs = line(oth, 1 - core, z, x, other_rows)
            for k in range(4):
                remote(theirs, theirs, fw_s.at[n, k], fw_r.at[n, k], sib_dev).wait_recv()
                remote(whole, whole, fw_s.at[n, k], fw_r.at[n, k], sib_dev).wait_send()
            for m in range(4, 8):
                gone = line(oth, core, z, x, rows, pl.ds(0, 4) if m % 2 == 0 else halves[0])
                remote(gone, gone, gat_s.at[n, m], gat_r.at[n, m], hop(core, 1)).wait_send()
        parts(emit)

    def exchange(n, src, dst, place, device, selfless):
        def send(k, carry):
            j = lax.rem(s + k, GROUP)
            remote(src.at[j], dst.at[place], a2a_s.at[n], a2a_r.at[n], device(j)).start()
            return carry

        if selfless is None:
            pltpu.make_async_copy(src.at[s], dst.at[s], a2a_r.at[n]).start()
        else:
            @pl.when(selfless)
            def _():
                pltpu.make_async_copy(src.at[s], dst.at[s], a2a_r.at[n]).start()

            @pl.when(jnp.logical_not(selfless))
            def _():
                send(0, 0)
        lax.fori_loop(1, GROUP, send, 0)

    def received(n, dst):
        remote(dst, dst, a2a_s.at[n], a2a_r.at[n], sib_dev).wait_recv()

    def sent(n, src, selfless):
        some = src.at[pl.ds(0, GROUP - 1)]
        remote(some, some, a2a_s.at[n], a2a_r.at[n], sib_dev).wait_send()
        if selfless is not None:
            @pl.when(jnp.logical_not(selfless))
            def _():
                one = src.at[0]
                remote(one, one, a2a_s.at[n], a2a_r.at[n], sib_dev).wait_send()

    def to_sibling(half, n, ref):
        return remote(
            ref.at[half, pl.ds(0, ROWS)], ref.at[half, pl.ds(ROWS, ROWS)],
            sib_s.at[half, n], sib_r.at[half, n], sib_dev,
        )

    frame = s - c + t

    gather_first(0, ws_own, ws_oth)

    def swap(n, own, ref):
        @pl.when(jnp.logical_not(stay))
        def _():
            remote(own, ref, swap_s.at[n], swap_r.at[n], swap_dev).start()

    swap(0, own_lat, x_lat)
    greet(plane_sem, z_line)
    for copy in local[3:]:
        copy.wait()
    m_adj[...] = own_adj[...].reshape(GROUP, SPAN, D)
    gather_second(0, ws_own, ws_oth)
    pl.semaphore_wait(plane_sem, 3)
    greet(all_sem, y_line)

    def arrive(n, own, ref):
        @pl.when(stay)
        def _():
            ref[...] = own[...]

        @pl.when(jnp.logical_not(stay))
        def _():
            remote(own, ref, swap_s.at[n], swap_r.at[n], swap_dev).wait()

    arrive(0, own_lat, x_lat)
    swap(1, own_prb, x_prb)
    gather_third(0, ws_oth)
    hid[0] = norm_stats(x_lat[...].astype(F32))[0].astype(BF)

    def project(half, w, slot, q_ref, k_ref, v_ref, q_scale, exchange_rows):
        hidden = hid[slot]
        lanes = pl.ds(0, HALF)
        rows = pl.ds(0, ROWS)
        key = nt(hidden, weight(w, 1))
        k_ref[half, rows, lanes] = key.astype(BF)
        if exchange_rows is not None:
            to_sibling(half, exchange_rows, k_ref).start()
        v_ref[half, rows, lanes] = nt(hidden, weight(w, 2)).astype(BF)
        if exchange_rows is not None:
            to_sibling(half, exchange_rows + 1, v_ref).start()
        q_ref[half, rows, lanes] = nt(hidden, weight(w, 0)).astype(BF)

    def spatial_heads(half, first, last):
        if first == 0:
            mix[half] = jnp.zeros((ROWS, PAD), F32)

        def body(h, carry):
            win, mask = head_window(h)
            k = keep(mask, sk[half, :, win])
            scores = nt(sq[half, :, win], k)
            e = jnp.exp2((scores - jnp.max(scores, axis=-1, keepdims=True)) * EXP2)
            p = e * (1.0 / jnp.sum(e, axis=-1, keepdims=True))
            w = p.astype(BF)
            probs[half * 8 + h] = w
            mix[half, :, win] += nn(w, keep(mask, sv[half, :, win]))
            return carry

        lax.fori_loop(first, last, body, 0)

    def tangent_heads(half, first, last, key_count, q_ref, k_ref, v_ref, dq_ref, dk_ref, dv_ref, p_ref):
        keys = pl.ds(0, key_count)
        if first == 0:
            dmix[half] = jnp.zeros((ROWS, PAD), F32)

        def body(h, carry):
            win, mask = head_window(h)
            k = keep(mask, k_ref[half, keys, win])
            dk = keep(mask, dk_ref[half, keys, win])
            ds = nt(dq_ref[half, :, win], k) + nt(q_ref[half, :, win], dk)
            w = p_ref[half * 8 + h]
            p = w.astype(F32)
            pd = p * (ds * SCALE)
            dp = (pd - p * jnp.sum(pd, axis=-1, keepdims=True)).astype(BF)
            out = nn(dp, keep(mask, v_ref[half, keys, win]))
            out += nn(w, keep(mask, dv_ref[half, keys, win]))
            dmix[half, :, win] += out
            return carry

        lax.fori_loop(first, last, body, 0)

    def out_proj(mixed, w_own, w_oth):
        lanes = pl.ds(0, HALF)
        first = nn(mixed[0, :, lanes].astype(BF), weight(w_own, 3))
        return first + nn(mixed[1, :, lanes].astype(BF), weight(w_oth, 3))

    def siblings(half, pairs):
        for n, ref in pairs:
            to_sibling(half, n, ref).wait()

    primal, moving = ((0, sk), (1, sv)), ((2, sdk), (3, sdv))
    spatial = (2 * ROWS, sq, sk, sv, sdq, sdk, sdv, probs)
    temporal = (ROWS, tq, tk, tv, sdq, sdk, sdv, tprobs)

    project(0, ws_own, 0, sq, sk, sv, None, 0)
    siblings(0, primal)
    spatial_heads(0, 0, 4)
    gather_fourth(0, ws_oth)
    spatial_heads(0, 4, 8)
    gather_fifth(0, ws_oth)

    arrive(1, own_prb, x_prb)
    gather_first(1, wt_own, wt_oth)
    normed, inverse = norm_stats(x_lat[...].astype(F32))
    hid[1] = norm_tangent(normed, inverse, x_prb[...].astype(F32)).astype(BF)
    project(0, ws_own, 1, sdq, sdk, sdv, None, 2)
    siblings(0, moving)
    tangent_heads(0, 0, 8, *spatial)
    gather_last(0, ws_oth)
    pl.semaphore_wait(all_sem, 7)
    exchange(1, m_adj, r_adj, s, lambda j: (j, t), None)

    project(1, ws_oth, 0, sq, sk, sv, None, 0)
    gather_second(1, wt_own, wt_oth)
    siblings(1, primal)
    spatial_heads(1, 0, 8)
    inner = (x_lat[...].astype(F32) + out_proj(mix, ws_own, ws_oth)).astype(BF)
    m_inner[...] = inner.reshape(GROUP, SPAN, D)
    exchange(0, m_inner, r_inner, frame, lambda j: (j, c), stay)
    gather_third(1, wt_oth)
    project(1, ws_oth, 1, sdq, sdk, sdv, None, 2)
    siblings(1, moving)
    tangent_heads(1, 0, 8, *spatial)
    gather_fourth(1, wt_oth)
    moved = out_proj(dmix, ws_own, ws_oth)
    tangent = x_prb[...].astype(F32)
    tr_out[...] = jnp.broadcast_to(mean(tangent * moved), (ROWS, 128))
    m_tan[...] = (tangent + moved).astype(BF).reshape(GROUP, SPAN, D)
    exchange(2, m_tan, r_tan, frame, lambda j: (j, c), stay)

    row = lax.broadcasted_iota(jnp.int32, (ROWS, ROWS), 0)
    col = lax.broadcasted_iota(jnp.int32, (ROWS, ROWS), 1)
    same = lax.rem(row, SPAN) == lax.rem(col, SPAN)

    received(0, r_inner)
    x_inner = r_inner[...].reshape(ROWS, D).astype(F32)
    hid[0] = norm_stats(x_inner)[0].astype(BF)
    received(1, r_adj)

    def back_lanes(half, w, g):
        gm = nt(g, weight(w, 3)).astype(BF)
        sdq[half, :, pl.ds(0, HALF)] = gm

    def temporal_heads(half):
        mix[half] = jnp.zeros((ROWS, PAD), F32)
        gq[...] = jnp.zeros(gq.shape, F32)
        gk[...] = jnp.zeros(gk.shape, F32)
        gv[...] = jnp.zeros(gv.shape, F32)

        def body(h, carry):
            win, mask = head_window(h)
            q = tq[half, :, win]
            k = keep(mask, tk[half, :, win])
            v = keep(mask, tv[half, :, win])
            g = sdq[half, :, win]
            scores = jnp.where(same, nt(q, k), -1e30)
            e = jnp.exp2((scores - jnp.max(scores, axis=-1, keepdims=True)) * EXP2)
            p = e * (1.0 / jnp.sum(e, axis=-1, keepdims=True))
            w = p.astype(BF)
            tprobs[half * 8 + h] = w
            mix[half, :, win] += nn(w, v)
            gw = nt(g, v)
            pg = p * (gw * SCALE)
            gs = (pg - p * jnp.sum(pg, axis=-1, keepdims=True)).astype(BF)
            gq[:, win] += nn(gs, k)
            gk[pl.ds(0, ROWS), win] += tn(gs, keep(mask, q))
            gv[pl.ds(0, ROWS), win] += tn(w, keep(mask, g))
            return carry

        lax.fori_loop(0, 8, body, 0)

    def hidden_back(w):
        lanes = pl.ds(0, HALF)
        rows = pl.ds(0, ROWS)
        out = nn(gq[:, lanes].astype(BF), weight(w, 0))
        out += nn(gk[rows, lanes].astype(BF), weight(w, 1))
        return out + nn(gv[rows, lanes].astype(BF), weight(w, 2))

    g_two = r_adj[...].reshape(ROWS, D)
    project(0, wt_own, 0, tq, tk, tv, None, None)
    back_lanes(0, wt_own, g_two)
    temporal_heads(0)
    gather_fifth(1, wt_oth)
    gh[...] = hidden_back(wt_own)
    gather_last(1, wt_oth)
    project(1, wt_oth, 0, tq, tk, tv, None, None)
    back_lanes(1, wt_oth, r_adj[...].reshape(ROWS, D))
    temporal_heads(1)
    g_hidden = gh[...] + hidden_back(wt_oth)
    normed, inverse = norm_stats(r_inner[...].reshape(ROWS, D).astype(F32))
    grad_two = norm_back(normed, inverse, g_hidden).astype(BF).astype(F32)
    grads_one = (r_adj[...].reshape(ROWS, D).astype(F32) + grad_two).astype(BF)
    m_g[...] = grads_one.reshape(GROUP, SPAN, D)
    exchange(
        3, m_g, r_g, s, lambda f: (lax.div(f, 2) * 2 + t, lax.rem(f, 2)), stay
    )
    reached = r_inner[...].reshape(ROWS, D).astype(F32) + out_proj(mix, wt_own, wt_oth)
    m_u[...] = reached.astype(BF).reshape(GROUP, SPAN, D)

    received(2, r_tan)
    normed, inverse = norm_stats(r_inner[...].reshape(ROWS, D).astype(F32))
    hid[1] = norm_tangent(normed, inverse, r_tan[...].reshape(ROWS, D).astype(F32)).astype(BF)
    project(0, wt_own, 1, sdq, sdk, sdv, None, None)
    project(1, wt_oth, 1, sdq, sdk, sdv, None, None)
    for half in range(2):
        tangent_heads(half, 0, 8, *temporal)
    m_d[...] = out_proj(dmix, wt_own, wt_oth).astype(BF).reshape(GROUP, SPAN, D)

    received(3, r_g)
    exchange(4, m_u, r_u, s, lambda f: (f, t), None)
    exchange(5, m_d, r_d, s, lambda f: (f, t), None)

    def spatial_back(half):
        gq[...] = jnp.zeros(gq.shape, F32)
        gk[...] = jnp.zeros(gk.shape, F32)
        gv[...] = jnp.zeros(gv.shape, F32)

        def body(h, carry):
            win, mask = head_window(h)
            g = sdq[half, :, win]
            w = probs[half * 8 + h]
            p = w.astype(F32)
            gw = nt(g, keep(mask, sv[half, :, win]))
            pg = p * (gw * SCALE)
            gs = (pg - p * jnp.sum(pg, axis=-1, keepdims=True)).astype(BF)
            gq[:, win] += nn(gs, keep(mask, sk[half, :, win]))
            gk[:, win] += tn(gs, keep(mask, sq[half, :, win]))
            gv[:, win] += tn(w, keep(mask, g))
            return carry

        lax.fori_loop(0, 8, body, 0)

    def key_back(half):
        return remote(
            gsib_out.at[half], gsib_in.at[half], gs_s.at[half], gs_r.at[half], sib_dev
        )

    for half, w in ((0, ws_own), (1, ws_oth)):
        back_lanes(half, w, r_g[...].reshape(ROWS, D))
        spatial_back(half)
        gsib_out[half, 0] = gk[pl.ds(ROWS, ROWS), :].astype(BF)
        gsib_out[half, 1] = gv[pl.ds(ROWS, ROWS), :].astype(BF)
        key_back(half).start()
        lanes = pl.ds(0, HALF)
        part = nn(gq[:, lanes].astype(BF), weight(w, 0))
        if half == 0:
            gh[...] = part
        else:
            gh[...] += part
        key_back(half).wait()
        rows = pl.ds(0, ROWS)
        key = gk[rows, lanes] + gsib_in[half, 0, :, lanes].astype(F32)
        value = gv[rows, lanes] + gsib_in[half, 1, :, lanes].astype(F32)
        part = nn(key.astype(BF), weight(w, 1)) + nn(value.astype(BF), weight(w, 2))
        gh[...] += part
    normed, inverse = norm_stats(x_lat[...].astype(F32))
    grad_one = norm_back(normed, inverse, gh[...])
    v_out[...] = (grad_one + r_g[...].reshape(ROWS, D).astype(F32)).astype(BF)

    @pl.when(jnp.logical_not(stay))
    def _():
        remote(v_out, v_in, end_s.at[0], end_r.at[0], swap_dev).start()
        remote(tr_out, tr_in, end_s.at[1], end_r.at[1], swap_dev).start()

    @pl.when(stay)
    def _():
        v_in[...] = v_out[...]
        tr_in[...] = tr_out[...]

    received(4, r_u)
    o_reached[...] = r_u[...].reshape(ROWS, D)
    received(5, r_d)
    extra = mean(own_prb[...].astype(F32) * r_d[...].reshape(ROWS, D).astype(F32))
    for n, ref, selfless in (
        (0, m_inner, stay), (1, m_adj, None), (2, m_tan, stay),
        (3, m_g, stay), (4, m_u, None), (5, m_d, None),
    ):
        sent(n, ref, selfless)

    @pl.when(jnp.logical_not(stay))
    def _():
        remote(v_out, v_in, end_s.at[0], end_r.at[0], swap_dev).wait()
        remote(tr_out, tr_in, end_s.at[1], end_r.at[1], swap_dev).wait()

    o_trace[...] = jnp.transpose(tr_in[...] + extra)[0:8]
    o_grads[...] = v_in[...]


def local(latent, probe, adjoint, spatial_qkv, spatial_proj, temporal_qkv, temporal_proj):
    def qkv(w):
        return jnp.transpose(w, (1, 2, 0)).reshape(3, 4, 144, D)

    def proj(w):
        return w.reshape(4, 144, D)

    dma = pltpu.SemaphoreType.DMA
    rows = pltpu.VMEM((ROWS, D), BF)
    weights = pltpu.VMEM((4, 4, 144, D), BF)
    one = pltpu.VMEM((2, ROWS, PAD), BF)
    two = pltpu.VMEM((2, 2 * ROWS, PAD), BF)
    message = pltpu.VMEM((GROUP, SPAN, D), BF)
    scratch = (
        [weights] * 4
        + [rows] * 5
        + [pltpu.VMEM((2, ROWS, D), BF)]
        + [one, two, two, one, two, two]
        + [pltpu.VMEM((16, ROWS, 2 * ROWS), BF)]
        + [one] * 3
        + [pltpu.VMEM((16, ROWS, ROWS), BF)]
        + [pltpu.VMEM((2, ROWS, PAD), F32)] * 2
        + [pltpu.VMEM((ROWS, PAD), F32)]
        + [pltpu.VMEM((2 * ROWS, PAD), F32)] * 2
        + [pltpu.VMEM((2, 2, ROWS, PAD), BF)] * 2
        + [pltpu.VMEM((ROWS, D), F32)]
        + [message] * 12
        + [rows] * 2
        + [pltpu.VMEM((ROWS, 128), F32)] * 2
        + [dma((3,)), dma((4,)), dma((2,)), dma((2,)), dma((2, 4)), dma((2, 4))]
        + [dma((2, 8)), dma((2, 8)), dma((2, 4)), dma((2, 4))]
        + [dma((6,)), dma((6,)), dma((2,)), dma((2,)), dma((2,)), dma((2,))]
        + [pltpu.SemaphoreType.REGULAR] * 2
    )
    reached, grads, trace = pl.pallas_call(
        kernel,
        out_shape=(
            jax.ShapeDtypeStruct((ROWS, D), BF),
            jax.ShapeDtypeStruct((ROWS, D), BF),
            jax.ShapeDtypeStruct((8, ROWS), F32),
        ),
        in_specs=[pl.BlockSpec(memory_space=pl.ANY)] * 7,
        out_specs=[pl.BlockSpec(memory_space=pltpu.VMEM)] * 3,
        scratch_shapes=scratch,
        compiler_params=pltpu.CompilerParams(
            collective_id=0, has_side_effects=True, vmem_limit_bytes=63 << 20
        ),
    )(
        latent, probe, adjoint,
        qkv(spatial_qkv), proj(spatial_proj), qkv(temporal_qkv), proj(temporal_proj),
    )
    new_latent = (0.5 * (latent.astype(F32) + reached[None].astype(F32))).astype(BF)
    new_adjoint = 1.5 * adjoint.astype(F32) - 0.5 * grads[None].astype(F32)
    return new_latent, new_adjoint, trace[0:1]


def solution(mesh):
    in_specs = (
        P("seq", "tp", None),
        P("seq", "tp", None),
        P("seq", "tp", None),
        P(None, None, "tp"),
        P("tp", None),
        P(None, None, "tp"),
        P("tp", None),
    )
    out_specs = (P("seq", "tp", None), P("seq", "tp", None), P("seq", "tp"))
    return jax.shard_map(local, mesh=mesh, in_specs=in_specs, out_specs=out_specs, check_vma=False)
```

```python
import jax
import jax.numpy as jnp
from jax import lax
from jax.experimental import pallas as pl
from jax.experimental.pallas import tpu as pltpu
from jax.sharding import PartitionSpec as P

MESH = pl.DeviceIdType.MESH
BF = jnp.bfloat16
F32 = jnp.float32

epsilon = 1e-06
HEAD = 72
D = 1152
ROWS = 256
HALF = 576
PAD = 640
WIN = 256
GROUP = 64
SPAN = 4
SCALE = HEAD ** (-0.5)
EXP2 = SCALE * 1.4426950408889634


def nt(a, b):
    return lax.dot_general(a, b, (((1,), (1,)), ((), ())), preferred_element_type=F32)


def nn(a, b):
    return lax.dot_general(a, b, (((1,), (0,)), ((), ())), preferred_element_type=F32)


def tn(a, b):
    return lax.dot_general(a, b, (((0,), (0,)), ((), ())), preferred_element_type=F32)


def mean(v):
    return jnp.sum(v, axis=-1, keepdims=True) * (1.0 / D)


def norm_stats(x):
    centred = x - mean(x)
    inverse = lax.rsqrt(mean(centred * centred) + epsilon)
    return centred * inverse, inverse


def norm_tangent(normed, inverse, t):
    centred = t - mean(t)
    return inverse * (centred - normed * mean(normed * centred))


def norm_back(normed, inverse, g):
    return inverse * (g - mean(g) - normed * mean(normed * g))


def weight(ref, kind):
    return ref[kind].reshape(HALF, D)


def head_window(h):
    block = jnp.minimum(lax.div(h * 9, 16), 3)
    base = pl.multiple_of(block * 128, 128)
    lane = lax.broadcasted_iota(jnp.int32, (1, WIN), 1) + block * 128
    return pl.ds(base, WIN), (lane >= h * HEAD) & (lane < h * HEAD + HEAD)


def keep(mask, v):
    return jnp.where(mask, v, jnp.zeros_like(v))


def rank():
    s, t = lax.axis_index("seq"), lax.axis_index("tp")
    return s, t, lax.rem(s, 2)


def kernel(
    latent, probe, adjoint, wsq, wsp, wtq, wtp,
    o_reached, o_grads, o_trace,
    ws_own, ws_oth, wt_own, wt_oth,
    own_lat, own_prb, own_adj, x_lat, x_prb,
    hid, sq, sk, sv, sdq, sdk, sdv, probs,
    tq, tk, tv, tprobs,
    mix, dmix, gq, gk, gv, gsib_out, gsib_in, gh,
    m_inner, m_tan, m_adj, r_inner, r_tan, r_adj,
    m_g, m_u, m_d, r_g, r_u, r_d,
    v_out, v_in, tr_out, tr_in,
    l_sem, w_sem, swap_s, swap_r, sib_s, sib_r,
    gat_s, gat_r, fw_s, fw_r, a2a_s, a2a_r, gs_s, gs_r, end_s, end_r, plane_sem, all_sem,
):
    s, t, c = rank()
    zx = lax.div(s, 4)
    z, x = lax.div(zx, 4), lax.rem(zx, 4)
    low = lax.rem(s, 4)
    stay = c == t
    swap_dev = (s - c + t, c)
    sib_dev = (s + 1 - 2 * c, t)
    y_dev = (s + 2 - 4 * lax.rem(lax.div(s, 2), 2), 1 - t)

    def remote(src, dst, ss, rs, dev):
        return pltpu.make_async_remote_copy(
            src_ref=src, dst_ref=dst, send_sem=ss, recv_sem=rs, device_id=dev, device_id_type=MESH
        )

    local = [
        pltpu.make_async_copy(wsq, ws_own.at[pl.ds(0, 3)], w_sem.at[0]),
        pltpu.make_async_copy(wsp, ws_own.at[3], w_sem.at[1]),
        pltpu.make_async_copy(latent.at[0], own_lat, l_sem.at[0]),
        pltpu.make_async_copy(probe.at[0], own_prb, l_sem.at[1]),
        pltpu.make_async_copy(adjoint.at[0], own_adj, l_sem.at[2]),
        pltpu.make_async_copy(wtq, wt_own.at[pl.ds(0, 3)], w_sem.at[2]),
        pltpu.make_async_copy(wtp, wt_own.at[3], w_sem.at[3]),
    ]
    for copy in local:
        copy.start()
    y_line = [
        (zx * 4 + lax.div(lax.rem(low * 2 + t + k, 8), 2), lax.rem(low * 2 + t + k, 2))
        for k in range(1, 8)
    ]
    x_line = [(z * 16 + lax.rem(x + k, 4) * 4 + low, t) for k in range(1, 4)]
    z_line = [(lax.rem(z + k, 4) * 16 + x * 4 + low, t) for k in range(1, 4)]

    def greet(sem, devices):
        for dev in devices:
            pl.semaphore_signal(sem, inc=1, device_id=dev, device_id_type=MESH)

    barrier = pltpu.get_barrier_semaphore()
    greet(barrier, y_line + x_line + z_line)
    for ref in (sq, sdq, tq):
        ref[:, :, pl.ds(HALF, PAD - HALF)] = jnp.zeros((2, ROWS, PAD - HALF), BF)
    for copy in local[:3]:
        copy.wait()
    pl.semaphore_wait(barrier, 13)

    def parts(emit):
        for core, first, size in ((0, 0, 80), (1, 80, 64)):
            @pl.when(c == core)
            def _(core=core, first=first, size=size):
                emit(core, pl.ds(first, size), size)

    def line(ref, core, i, j, rows, some=pl.ds(0, 4)):
        if core == 0:
            return ref.at[i, some, rows, :]
        return ref.at[some, j, rows, :]

    def hop(core, k):
        if core == 0:
            return (lax.rem(z + k, 4) * 16 + x * 4 + low, t)
        return (z * 16 + lax.rem(x + k, 4) * 4 + low, t)

    def step(core, k):
        if core == 0:
            return (z * 16 + lax.rem(x + k, 4) * 4 + low, t)
        return (lax.rem(z + k, 4) * 16 + x * 4 + low, t)

    def gather_first(n, own, oth):
        def emit(core, rows, size):
            remote(
                own.at[z, x, rows, :], oth.at[z, x, rows, :],
                gat_s.at[n, 0], gat_r.at[n, 0], y_dev,
            ).start()
        parts(emit)

    def gather_second(n, own, oth):
        def emit(core, rows, size):
            remote(
                own.at[z, x, rows, :], oth.at[z, x, rows, :],
                gat_s.at[n, 0], gat_r.at[n, 0], y_dev,
            ).wait()
            for k in range(1, 4):
                remote(
                    oth.at[z, x, rows, :], oth.at[z, x, rows, :],
                    gat_s.at[n, k], gat_r.at[n, k], step(core, k),
                ).start()
        parts(emit)

    halves = (pl.ds(0, 2), pl.ds(2, 2))

    def gather_third(n, oth):
        def emit(core, rows, size):
            for k in range(1, 4):
                remote(
                    oth.at[z, x, rows, :], oth.at[z, x, rows, :],
                    gat_s.at[n, k], gat_r.at[n, k], step(core, k),
                ).wait()
            whole = line(oth, core, z, x, rows)
            for k, m in ((1, 4), (3, 6)):
                remote(whole, whole, gat_s.at[n, m], gat_r.at[n, m], hop(core, k)).start()
            remote(whole, whole, fw_s.at[n, 0], fw_r.at[n, 0], sib_dev).start()
        parts(emit)

    def gather_fourth(n, oth):
        def emit(core, rows, size):
            for k, m, some in ((1, 4, halves[0]), (3, 6, halves[1])):
                i, j = lax.rem(z - k + 4, 4), lax.rem(x - k + 4, 4)
                came = line(oth, core, i, j, rows)
                part = line(oth, core, i, j, rows, some)
                remote(came, came, gat_s.at[n, m], gat_r.at[n, m], hop(core, k)).wait_recv()
                remote(part, part, gat_s.at[n, m + 1], gat_r.at[n, m + 1], hop(core, k)).start()
                remote(came, came, fw_s.at[n, k], fw_r.at[n, k], sib_dev).start()
        parts(emit)

    def gather_fifth(n, oth):
        def emit(core, rows, size):
            i, j = lax.rem(z + 2, 4), lax.rem(x + 2, 4)
            for k, m, some in ((1, 5, halves[0]), (3, 7, halves[1])):
                part = line(oth, core, i, j, rows, some)
                remote(part, part, gat_s.at[n, m], gat_r.at[n, m], hop(core, k)).wait_recv()
            came = line(oth, core, i, j, rows)
            remote(came, came, fw_s.at[n, 2], fw_r.at[n, 2], sib_dev).start()
        parts(emit)

    def gather_last(n, oth):
        def emit(core, rows, size):
            whole = line(oth, core, z, x, rows)
            other_rows = pl.ds(80, 64) if core == 0 else pl.ds(0, 80)
            theirs = line(oth, 1 - core, z, x, other_rows)
            for k in range(4):
                remote(theirs, theirs, fw_s.at[n, k], fw_r.at[n, k], sib_dev).wait_recv()
                remote(whole, whole, fw_s.at[n, k], fw_r.at[n, k], sib_dev).wait_send()
            for m in range(4, 8):
                gone = line(oth, core, z, x, rows, pl.ds(0, 4) if m % 2 == 0 else halves[0])
                remote(gone, gone, gat_s.at[n, m], gat_r.at[n, m], hop(core, 1)).wait_send()
        parts(emit)

    def exchange(n, src, dst, place, device, selfless):
        def send(k, carry):
            j = lax.rem(s + k, GROUP)
            remote(src.at[j], dst.at[place], a2a_s.at[n], a2a_r.at[n], device(j)).start()
            return carry

        if selfless is None:
            pltpu.make_async_copy(src.at[s], dst.at[s], a2a_r.at[n]).start()
        else:
            @pl.when(selfless)
            def _():
                pltpu.make_async_copy(src.at[s], dst.at[s], a2a_r.at[n]).start()

            @pl.when(jnp.logical_not(selfless))
            def _():
                send(0, 0)
        lax.fori_loop(1, GROUP, send, 0)

    def received(n, dst):
        remote(dst, dst, a2a_s.at[n], a2a_r.at[n], sib_dev).wait_recv()

    def sent(n, src, selfless):
        some = src.at[pl.ds(0, GROUP - 1)]
        remote(some, some, a2a_s.at[n], a2a_r.at[n], sib_dev).wait_send()
        if selfless is not None:
            @pl.when(jnp.logical_not(selfless))
            def _():
                one = src.at[0]
                remote(one, one, a2a_s.at[n], a2a_r.at[n], sib_dev).wait_send()

    def to_sibling(half, n, ref):
        return remote(
            ref.at[half, pl.ds(0, ROWS)], ref.at[half, pl.ds(ROWS, ROWS)],
            sib_s.at[half, n], sib_r.at[half, n], sib_dev,
        )

    frame = s - c + t

    gather_first(0, ws_own, ws_oth)

    def swap(n, own, ref):
        @pl.when(jnp.logical_not(stay))
        def _():
            remote(own, ref, swap_s.at[n], swap_r.at[n], swap_dev).start()

    swap(0, own_lat, x_lat)
    greet(plane_sem, z_line)
    for copy in local[3:]:
        copy.wait()
    m_adj[...] = own_adj[...].reshape(GROUP, SPAN, D)
    gather_second(0, ws_own, ws_oth)
    gather_first(1, wt_own, wt_oth)
    pl.semaphore_wait(plane_sem, 3)
    greet(all_sem, y_line)

    def arrive(n, own, ref):
        @pl.when(stay)
        def _():
            ref[...] = own[...]

        @pl.when(jnp.logical_not(stay))
        def _():
            remote(own, ref, swap_s.at[n], swap_r.at[n], swap_dev).wait()

    arrive(0, own_lat, x_lat)
    swap(1, own_prb, x_prb)
    gather_third(0, ws_oth)
    hid[0] = norm_stats(x_lat[...].astype(F32))[0].astype(BF)

    def project(half, w, slot, q_ref, k_ref, v_ref, q_scale, exchange_rows):
        hidden = hid[slot]
        lanes = pl.ds(0, HALF)
        rows = pl.ds(0, ROWS)
        key = nt(hidden, weight(w, 1))
        k_ref[half, rows, lanes] = key.astype(BF)
        if exchange_rows is not None:
            to_sibling(half, exchange_rows, k_ref).start()
        v_ref[half, rows, lanes] = nt(hidden, weight(w, 2)).astype(BF)
        if exchange_rows is not None:
            to_sibling(half, exchange_rows + 1, v_ref).start()
        q_ref[half, rows, lanes] = nt(hidden, weight(w, 0)).astype(BF)

    def spatial_heads(half, first, last):
        if first == 0:
            mix[half] = jnp.zeros((ROWS, PAD), F32)

        def body(h, carry):
            win, mask = head_window(h)
            k = keep(mask, sk[half, :, win])
            scores = nt(sq[half, :, win], k)
            e = jnp.exp2((scores - jnp.max(scores, axis=-1, keepdims=True)) * EXP2)
            p = e * (1.0 / jnp.sum(e, axis=-1, keepdims=True))
            w = p.astype(BF)
            probs[half * 8 + h] = w
            mix[half, :, win] += nn(w, keep(mask, sv[half, :, win]))
            return carry

        lax.fori_loop(first, last, body, 0, unroll=2)

    def tangent_heads(half, first, last, key_count, q_ref, k_ref, v_ref, dq_ref, dk_ref, dv_ref, p_ref):
        keys = pl.ds(0, key_count)
        if first == 0:
            dmix[half] = jnp.zeros((ROWS, PAD), F32)

        def body(h, carry):
            win, mask = head_window(h)
            k = keep(mask, k_ref[half, keys, win])
            dk = keep(mask, dk_ref[half, keys, win])
            ds = nt(dq_ref[half, :, win], k) + nt(q_ref[half, :, win], dk)
            w = p_ref[half * 8 + h]
            p = w.astype(F32)
            pd = p * (ds * SCALE)
            dp = (pd - p * jnp.sum(pd, axis=-1, keepdims=True)).astype(BF)
            out = nn(dp, keep(mask, v_ref[half, keys, win]))
            out += nn(w, keep(mask, dv_ref[half, keys, win]))
            dmix[half, :, win] += out
            return carry

        lax.fori_loop(first, last, body, 0, unroll=2)

    def out_proj(mixed, w_own, w_oth):
        lanes = pl.ds(0, HALF)
        first = nn(mixed[0, :, lanes].astype(BF), weight(w_own, 3))
        return first + nn(mixed[1, :, lanes].astype(BF), weight(w_oth, 3))

    def siblings(half, pairs):
        for n, ref in pairs:
            to_sibling(half, n, ref).wait()

    primal, moving = ((0, sk), (1, sv)), ((2, sdk), (3, sdv))
    spatial = (2 * ROWS, sq, sk, sv, sdq, sdk, sdv, probs)
    temporal = (ROWS, tq, tk, tv, sdq, sdk, sdv, tprobs)

    project(0, ws_own, 0, sq, sk, sv, None, 0)
    gather_second(1, wt_own, wt_oth)
    siblings(0, primal)
    spatial_heads(0, 0, 8)

    arrive(1, own_prb, x_prb)
    normed, inverse = norm_stats(x_lat[...].astype(F32))
    hid[1] = norm_tangent(normed, inverse, x_prb[...].astype(F32)).astype(BF)
    project(0, ws_own, 1, sdq, sdk, sdv, None, 2)
    gather_fourth(0, ws_oth)
    gather_third(1, wt_oth)
    siblings(0, moving)
    tangent_heads(0, 0, 4, *spatial)
    gather_fifth(0, ws_oth)
    pl.semaphore_wait(all_sem, 7)
    exchange(1, m_adj, r_adj, s, lambda j: (j, t), None)
    tangent_heads(0, 4, 8, *spatial)
    gather_last(0, ws_oth)

    project(1, ws_oth, 0, sq, sk, sv, None, 0)
    siblings(1, primal)
    spatial_heads(1, 0, 8)
    inner = (x_lat[...].astype(F32) + out_proj(mix, ws_own, ws_oth)).astype(BF)
    m_inner[...] = inner.reshape(GROUP, SPAN, D)
    exchange(0, m_inner, r_inner, frame, lambda j: (j, c), stay)
    gather_fourth(1, wt_oth)
    project(1, ws_oth, 1, sdq, sdk, sdv, None, 2)
    siblings(1, moving)
    tangent_heads(1, 0, 8, *spatial)
    gather_fifth(1, wt_oth)
    moved = out_proj(dmix, ws_own, ws_oth)
    tangent = x_prb[...].astype(F32)
    tr_out[...] = jnp.broadcast_to(mean(tangent * moved), (ROWS, 128))
    m_tan[...] = (tangent + moved).astype(BF).reshape(GROUP, SPAN, D)
    exchange(2, m_tan, r_tan, frame, lambda j: (j, c), stay)

    row = lax.broadcasted_iota(jnp.int32, (ROWS, ROWS), 0)
    col = lax.broadcasted_iota(jnp.int32, (ROWS, ROWS), 1)
    same = lax.rem(row, SPAN) == lax.rem(col, SPAN)

    received(0, r_inner)
    x_inner = r_inner[...].reshape(ROWS, D).astype(F32)
    hid[0] = norm_stats(x_inner)[0].astype(BF)
    received(1, r_adj)

    def back_lanes(half, w, g):
        gm = nt(g, weight(w, 3)).astype(BF)
        sdq[half, :, pl.ds(0, HALF)] = gm

    def temporal_heads(half):
        mix[half] = jnp.zeros((ROWS, PAD), F32)
        gq[...] = jnp.zeros(gq.shape, F32)
        gk[...] = jnp.zeros(gk.shape, F32)
        gv[...] = jnp.zeros(gv.shape, F32)

        def body(h, carry):
            win, mask = head_window(h)
            q = tq[half, :, win]
            k = keep(mask, tk[half, :, win])
            v = keep(mask, tv[half, :, win])
            g = sdq[half, :, win]
            scores = jnp.where(same, nt(q, k), -1e30)
            e = jnp.exp2((scores - jnp.max(scores, axis=-1, keepdims=True)) * EXP2)
            p = e * (1.0 / jnp.sum(e, axis=-1, keepdims=True))
            w = p.astype(BF)
            tprobs[half * 8 + h] = w
            mix[half, :, win] += nn(w, v)
            gw = nt(g, v)
            pg = p * (gw * SCALE)
            gs = (pg - p * jnp.sum(pg, axis=-1, keepdims=True)).astype(BF)
            gq[:, win] += nn(gs, k)
            gk[pl.ds(0, ROWS), win] += tn(gs, keep(mask, q))
            gv[pl.ds(0, ROWS), win] += tn(w, keep(mask, g))
            return carry

        lax.fori_loop(0, 8, body, 0, unroll=2)

    def hidden_back(w):
        lanes = pl.ds(0, HALF)
        rows = pl.ds(0, ROWS)
        out = nn(gq[:, lanes].astype(BF), weight(w, 0))
        out += nn(gk[rows, lanes].astype(BF), weight(w, 1))
        return out + nn(gv[rows, lanes].astype(BF), weight(w, 2))

    g_two = r_adj[...].reshape(ROWS, D)
    project(0, wt_own, 0, tq, tk, tv, None, None)
    back_lanes(0, wt_own, g_two)
    temporal_heads(0)
    gh[...] = hidden_back(wt_own)
    gather_last(1, wt_oth)
    project(1, wt_oth, 0, tq, tk, tv, None, None)
    back_lanes(1, wt_oth, r_adj[...].reshape(ROWS, D))
    temporal_heads(1)
    g_hidden = gh[...] + hidden_back(wt_oth)
    normed, inverse = norm_stats(r_inner[...].reshape(ROWS, D).astype(F32))
    grad_two = norm_back(normed, inverse, g_hidden).astype(BF).astype(F32)
    grads_one = (r_adj[...].reshape(ROWS, D).astype(F32) + grad_two).astype(BF)
    m_g[...] = grads_one.reshape(GROUP, SPAN, D)
    exchange(
        3, m_g, r_g, s, lambda f: (lax.div(f, 2) * 2 + t, lax.rem(f, 2)), stay
    )
    reached = r_inner[...].reshape(ROWS, D).astype(F32) + out_proj(mix, wt_own, wt_oth)
    m_u[...] = reached.astype(BF).reshape(GROUP, SPAN, D)

    received(2, r_tan)
    normed, inverse = norm_stats(r_inner[...].reshape(ROWS, D).astype(F32))
    hid[1] = norm_tangent(normed, inverse, r_tan[...].reshape(ROWS, D).astype(F32)).astype(BF)
    project(0, wt_own, 1, sdq, sdk, sdv, None, None)
    project(1, wt_oth, 1, sdq, sdk, sdv, None, None)
    for half in range(2):
        tangent_heads(half, 0, 8, *temporal)
    m_d[...] = out_proj(dmix, wt_own, wt_oth).astype(BF).reshape(GROUP, SPAN, D)

    received(3, r_g)
    exchange(4, m_u, r_u, s, lambda f: (f, t), None)
    exchange(5, m_d, r_d, s, lambda f: (f, t), None)

    def spatial_back(half):
        gq[...] = jnp.zeros(gq.shape, F32)
        gk[...] = jnp.zeros(gk.shape, F32)
        gv[...] = jnp.zeros(gv.shape, F32)

        def body(h, carry):
            win, mask = head_window(h)
            g = sdq[half, :, win]
            w = probs[half * 8 + h]
            p = w.astype(F32)
            gw = nt(g, keep(mask, sv[half, :, win]))
            pg = p * (gw * SCALE)
            gs = (pg - p * jnp.sum(pg, axis=-1, keepdims=True)).astype(BF)
            gq[:, win] += nn(gs, keep(mask, sk[half, :, win]))
            gk[:, win] += tn(gs, keep(mask, sq[half, :, win]))
            gv[:, win] += tn(w, keep(mask, g))
            return carry

        lax.fori_loop(0, 8, body, 0, unroll=2)

    def key_back(half):
        return remote(
            gsib_out.at[half], gsib_in.at[half], gs_s.at[half], gs_r.at[half], sib_dev
        )

    for half, w in ((0, ws_own), (1, ws_oth)):
        back_lanes(half, w, r_g[...].reshape(ROWS, D))
        spatial_back(half)
        gsib_out[half, 0] = gk[pl.ds(ROWS, ROWS), :].astype(BF)
        gsib_out[half, 1] = gv[pl.ds(ROWS, ROWS), :].astype(BF)
        key_back(half).start()
        lanes = pl.ds(0, HALF)
        part = nn(gq[:, lanes].astype(BF), weight(w, 0))
        if half == 0:
            gh[...] = part
        else:
            gh[...] += part
        key_back(half).wait()
        rows = pl.ds(0, ROWS)
        key = gk[rows, lanes] + gsib_in[half, 0, :, lanes].astype(F32)
        value = gv[rows, lanes] + gsib_in[half, 1, :, lanes].astype(F32)
        part = nn(key.astype(BF), weight(w, 1)) + nn(value.astype(BF), weight(w, 2))
        gh[...] += part
    normed, inverse = norm_stats(x_lat[...].astype(F32))
    grad_one = norm_back(normed, inverse, gh[...])
    v_out[...] = (grad_one + r_g[...].reshape(ROWS, D).astype(F32)).astype(BF)

    @pl.when(jnp.logical_not(stay))
    def _():
        remote(v_out, v_in, end_s.at[0], end_r.at[0], swap_dev).start()
        remote(tr_out, tr_in, end_s.at[1], end_r.at[1], swap_dev).start()

    @pl.when(stay)
    def _():
        v_in[...] = v_out[...]
        tr_in[...] = tr_out[...]

    received(4, r_u)
    o_reached[...] = r_u[...].reshape(ROWS, D)
    received(5, r_d)
    extra = mean(own_prb[...].astype(F32) * r_d[...].reshape(ROWS, D).astype(F32))
    for n, ref, selfless in (
        (0, m_inner, stay), (1, m_adj, None), (2, m_tan, stay),
        (3, m_g, stay), (4, m_u, None), (5, m_d, None),
    ):
        sent(n, ref, selfless)

    @pl.when(jnp.logical_not(stay))
    def _():
        remote(v_out, v_in, end_s.at[0], end_r.at[0], swap_dev).wait()
        remote(tr_out, tr_in, end_s.at[1], end_r.at[1], swap_dev).wait()

    o_trace[...] = jnp.transpose(tr_in[...] + extra)[0:8]
    o_grads[...] = v_in[...]


def local(latent, probe, adjoint, spatial_qkv, spatial_proj, temporal_qkv, temporal_proj):
    def qkv(w):
        return jnp.transpose(w, (1, 2, 0)).reshape(3, 4, 144, D)

    def proj(w):
        return w.reshape(4, 144, D)

    dma = pltpu.SemaphoreType.DMA
    rows = pltpu.VMEM((ROWS, D), BF)
    weights = pltpu.VMEM((4, 4, 144, D), BF)
    one = pltpu.VMEM((2, ROWS, PAD), BF)
    two = pltpu.VMEM((2, 2 * ROWS, PAD), BF)
    message = pltpu.VMEM((GROUP, SPAN, D), BF)
    scratch = (
        [weights] * 4
        + [rows] * 5
        + [pltpu.VMEM((2, ROWS, D), BF)]
        + [one, two, two, one, two, two]
        + [pltpu.VMEM((16, ROWS, 2 * ROWS), BF)]
        + [one] * 3
        + [pltpu.VMEM((16, ROWS, ROWS), BF)]
        + [pltpu.VMEM((2, ROWS, PAD), F32)] * 2
        + [pltpu.VMEM((ROWS, PAD), F32)]
        + [pltpu.VMEM((2 * ROWS, PAD), F32)] * 2
        + [pltpu.VMEM((2, 2, ROWS, PAD), BF)] * 2
        + [pltpu.VMEM((ROWS, D), F32)]
        + [message] * 12
        + [rows] * 2
        + [pltpu.VMEM((ROWS, 128), F32)] * 2
        + [dma((3,)), dma((4,)), dma((2,)), dma((2,)), dma((2, 4)), dma((2, 4))]
        + [dma((2, 8)), dma((2, 8)), dma((2, 4)), dma((2, 4))]
        + [dma((6,)), dma((6,)), dma((2,)), dma((2,)), dma((2,)), dma((2,))]
        + [pltpu.SemaphoreType.REGULAR] * 2
    )
    reached, grads, trace = pl.pallas_call(
        kernel,
        out_shape=(
            jax.ShapeDtypeStruct((ROWS, D), BF),
            jax.ShapeDtypeStruct((ROWS, D), BF),
            jax.ShapeDtypeStruct((8, ROWS), F32),
        ),
        in_specs=[pl.BlockSpec(memory_space=pl.ANY)] * 7,
        out_specs=[pl.BlockSpec(memory_space=pltpu.VMEM)] * 3,
        scratch_shapes=scratch,
        compiler_params=pltpu.CompilerParams(
            collective_id=0, has_side_effects=True, vmem_limit_bytes=63 << 20
        ),
    )(
        latent, probe, adjoint,
        qkv(spatial_qkv), proj(spatial_proj), qkv(temporal_qkv), proj(temporal_proj),
    )
    new_latent = (0.5 * (latent.astype(F32) + reached[None].astype(F32))).astype(BF)
    new_adjoint = 1.5 * adjoint.astype(F32) - 0.5 * grads[None].astype(F32)
    return new_latent, new_adjoint, trace[0:1]


def solution(mesh):
    in_specs = (
        P("seq", "tp", None),
        P("seq", "tp", None),
        P("seq", "tp", None),
        P(None, None, "tp"),
        P("tp", None),
        P(None, None, "tp"),
        P("tp", None),
    )
    out_specs = (P("seq", "tp", None), P("seq", "tp", None), P("seq", "tp"))
    return jax.shard_map(local, mesh=mesh, in_specs=in_specs, out_specs=out_specs, check_vma=False)
```

```python
import jax
import jax.numpy as jnp
from jax import lax
from jax.experimental import pallas as pl
from jax.experimental.pallas import tpu as pltpu
from jax.sharding import PartitionSpec as P

MESH = pl.DeviceIdType.MESH
BF = jnp.bfloat16
F32 = jnp.float32

epsilon = 1e-06
HEAD = 72
D = 1152
ROWS = 256
HALF = 576
PAD = 640
WIN = 256
GROUP = 64
SPAN = 4
SCALE = HEAD ** (-0.5)
EXP2 = SCALE * 1.4426950408889634


def nt(a, b):
    return lax.dot_general(a, b, (((1,), (1,)), ((), ())), preferred_element_type=F32)


def nn(a, b):
    return lax.dot_general(a, b, (((1,), (0,)), ((), ())), preferred_element_type=F32)


def tn(a, b):
    return lax.dot_general(a, b, (((0,), (0,)), ((), ())), preferred_element_type=F32)


def mean(v):
    return jnp.sum(v, axis=-1, keepdims=True) * (1.0 / D)


def norm_stats(x):
    centred = x - mean(x)
    inverse = lax.rsqrt(mean(centred * centred) + epsilon)
    return centred * inverse, inverse


def norm_tangent(normed, inverse, t):
    centred = t - mean(t)
    return inverse * (centred - normed * mean(normed * centred))


def norm_back(normed, inverse, g):
    return inverse * (g - mean(g) - normed * mean(normed * g))


def weight(ref, kind):
    return ref[kind].reshape(HALF, D)


def head_window(h):
    block = jnp.minimum(lax.div(h * 9, 16), 3)
    base = pl.multiple_of(block * 128, 128)
    lane = lax.broadcasted_iota(jnp.int32, (1, WIN), 1) + block * 128
    return pl.ds(base, WIN), (lane >= h * HEAD) & (lane < h * HEAD + HEAD)


def keep(mask, v):
    return jnp.where(mask, v, jnp.zeros_like(v))


def rank():
    s, t = lax.axis_index("seq"), lax.axis_index("tp")
    return s, t, lax.rem(s, 2)


def kernel(
    latent, probe, adjoint, wsq, wsp, wtq, wtp,
    o_reached, o_grads, o_trace,
    ws_own, ws_oth, wt_own, wt_oth,
    own_lat, own_prb, own_adj, x_lat, x_prb,
    hid, sq, sk, sv, sdq, sdk, sdv, probs,
    tq, tk, tv, tprobs,
    mix, dmix, gq, gk, gv, gsib_out, gsib_in, gh,
    m_inner, m_tan, m_adj, r_inner, r_tan, r_adj,
    m_g, m_u, m_d, r_g, r_u, r_d,
    v_out, v_in, tr_out, tr_in,
    l_sem, w_sem, swap_s, swap_r, sib_s, sib_r,
    gat_s, gat_r, fw_s, fw_r, a2a_s, a2a_r, gs_s, gs_r, end_s, end_r, plane_sem, all_sem,
):
    s, t, c = rank()
    zx = lax.div(s, 4)
    z, x = lax.div(zx, 4), lax.rem(zx, 4)
    low = lax.rem(s, 4)
    stay = c == t
    swap_dev = (s - c + t, c)
    sib_dev = (s + 1 - 2 * c, t)
    y_dev = (s + 2 - 4 * lax.rem(lax.div(s, 2), 2), 1 - t)

    def remote(src, dst, ss, rs, dev):
        return pltpu.make_async_remote_copy(
            src_ref=src, dst_ref=dst, send_sem=ss, recv_sem=rs, device_id=dev, device_id_type=MESH
        )

    local = [
        pltpu.make_async_copy(wsq, ws_own.at[pl.ds(0, 3)], w_sem.at[0]),
        pltpu.make_async_copy(wsp, ws_own.at[3], w_sem.at[1]),
        pltpu.make_async_copy(latent.at[0], own_lat, l_sem.at[0]),
        pltpu.make_async_copy(probe.at[0], own_prb, l_sem.at[1]),
        pltpu.make_async_copy(adjoint.at[0], own_adj, l_sem.at[2]),
        pltpu.make_async_copy(wtq, wt_own.at[pl.ds(0, 3)], w_sem.at[2]),
        pltpu.make_async_copy(wtp, wt_own.at[3], w_sem.at[3]),
    ]
    for copy in local:
        copy.start()
    y_line = [
        (zx * 4 + lax.div(lax.rem(low * 2 + t + k, 8), 2), lax.rem(low * 2 + t + k, 2))
        for k in range(1, 8)
    ]
    x_line = [(z * 16 + lax.rem(x + k, 4) * 4 + low, t) for k in range(1, 4)]
    z_line = [(lax.rem(z + k, 4) * 16 + x * 4 + low, t) for k in range(1, 4)]

    def greet(sem, devices):
        for dev in devices:
            pl.semaphore_signal(sem, inc=1, device_id=dev, device_id_type=MESH)

    barrier = pltpu.get_barrier_semaphore()
    greet(barrier, y_line + x_line + z_line)
    for ref in (sq, sdq, tq):
        ref[:, :, pl.ds(HALF, PAD - HALF)] = jnp.zeros((2, ROWS, PAD - HALF), BF)
    for copy in local[:3]:
        copy.wait()
    pl.semaphore_wait(barrier, 13)

    def parts(emit):
        for core, first, size in ((0, 0, 80), (1, 80, 64)):
            @pl.when(c == core)
            def _(core=core, first=first, size=size):
                emit(core, pl.ds(first, size), size)

    def line(ref, core, i, j, rows, some=pl.ds(0, 4)):
        if core == 0:
            return ref.at[i, some, rows, :]
        return ref.at[some, j, rows, :]

    def hop(core, k):
        if core == 0:
            return (lax.rem(z + k, 4) * 16 + x * 4 + low, t)
        return (z * 16 + lax.rem(x + k, 4) * 4 + low, t)

    def step(core, k):
        if core == 0:
            return (z * 16 + lax.rem(x + k, 4) * 4 + low, t)
        return (lax.rem(z + k, 4) * 16 + x * 4 + low, t)

    def gather_first(n, own, oth):
        def emit(core, rows, size):
            remote(
                own.at[z, x, rows, :], oth.at[z, x, rows, :],
                gat_s.at[n, 0], gat_r.at[n, 0], y_dev,
            ).start()
        parts(emit)

    def gather_second(n, own, oth):
        def emit(core, rows, size):
            remote(
                own.at[z, x, rows, :], oth.at[z, x, rows, :],
                gat_s.at[n, 0], gat_r.at[n, 0], y_dev,
            ).wait()
            for k in range(1, 4):
                remote(
                    oth.at[z, x, rows, :], oth.at[z, x, rows, :],
                    gat_s.at[n, k], gat_r.at[n, k], step(core, k),
                ).start()
        parts(emit)

    halves = (pl.ds(0, 2), pl.ds(2, 2))

    def gather_third(n, oth):
        def emit(core, rows, size):
            for k in range(1, 4):
                remote(
                    oth.at[z, x, rows, :], oth.at[z, x, rows, :],
                    gat_s.at[n, k], gat_r.at[n, k], step(core, k),
                ).wait()
            whole = line(oth, core, z, x, rows)
            for k, m in ((1, 4), (3, 6)):
                remote(whole, whole, gat_s.at[n, m], gat_r.at[n, m], hop(core, k)).start()
            remote(whole, whole, fw_s.at[n, 0], fw_r.at[n, 0], sib_dev).start()
        parts(emit)

    def gather_fourth(n, oth):
        def emit(core, rows, size):
            for k, m, some in ((1, 4, halves[0]), (3, 6, halves[1])):
                i, j = lax.rem(z - k + 4, 4), lax.rem(x - k + 4, 4)
                came = line(oth, core, i, j, rows)
                part = line(oth, core, i, j, rows, some)
                remote(came, came, gat_s.at[n, m], gat_r.at[n, m], hop(core, k)).wait_recv()
                remote(part, part, gat_s.at[n, m + 1], gat_r.at[n, m + 1], hop(core, k)).start()
                remote(came, came, fw_s.at[n, k], fw_r.at[n, k], sib_dev).start()
        parts(emit)

    def gather_fifth(n, oth):
        def emit(core, rows, size):
            i, j = lax.rem(z + 2, 4), lax.rem(x + 2, 4)
            for k, m, some in ((1, 5, halves[0]), (3, 7, halves[1])):
                part = line(oth, core, i, j, rows, some)
                remote(part, part, gat_s.at[n, m], gat_r.at[n, m], hop(core, k)).wait_recv()
            came = line(oth, core, i, j, rows)
            remote(came, came, fw_s.at[n, 2], fw_r.at[n, 2], sib_dev).start()
        parts(emit)

    def gather_last(n, oth):
        def emit(core, rows, size):
            whole = line(oth, core, z, x, rows)
            other_rows = pl.ds(80, 64) if core == 0 else pl.ds(0, 80)
            theirs = line(oth, 1 - core, z, x, other_rows)
            for k in range(4):
                remote(theirs, theirs, fw_s.at[n, k], fw_r.at[n, k], sib_dev).wait_recv()
                remote(whole, whole, fw_s.at[n, k], fw_r.at[n, k], sib_dev).wait_send()
            for m in range(4, 8):
                gone = line(oth, core, z, x, rows, pl.ds(0, 4) if m % 2 == 0 else halves[0])
                remote(gone, gone, gat_s.at[n, m], gat_r.at[n, m], hop(core, 1)).wait_send()
        parts(emit)

    def exchange(n, src, dst, place, device, selfless):
        def send(k, carry):
            j = lax.rem(s + k, GROUP)
            remote(src.at[j], dst.at[place], a2a_s.at[n], a2a_r.at[n], device(j)).start()
            return carry

        if selfless is None:
            pltpu.make_async_copy(src.at[s], dst.at[s], a2a_r.at[n]).start()
        else:
            @pl.when(selfless)
            def _():
                pltpu.make_async_copy(src.at[s], dst.at[s], a2a_r.at[n]).start()

            @pl.when(jnp.logical_not(selfless))
            def _():
                send(0, 0)
        lax.fori_loop(1, GROUP, send, 0)

    def received(n, dst):
        remote(dst, dst, a2a_s.at[n], a2a_r.at[n], sib_dev).wait_recv()

    def sent(n, src, selfless):
        some = src.at[pl.ds(0, GROUP - 1)]
        remote(some, some, a2a_s.at[n], a2a_r.at[n], sib_dev).wait_send()
        if selfless is not None:
            @pl.when(jnp.logical_not(selfless))
            def _():
                one = src.at[0]
                remote(one, one, a2a_s.at[n], a2a_r.at[n], sib_dev).wait_send()

    def to_sibling(half, n, ref):
        return remote(
            ref.at[half, pl.ds(0, ROWS)], ref.at[half, pl.ds(ROWS, ROWS)],
            sib_s.at[half, n], sib_r.at[half, n], sib_dev,
        )

    frame = s - c + t

    gather_first(0, ws_own, ws_oth)

    def swap(n, own, ref):
        @pl.when(jnp.logical_not(stay))
        def _():
            remote(own, ref, swap_s.at[n], swap_r.at[n], swap_dev).start()

    swap(0, own_lat, x_lat)
    greet(plane_sem, z_line)
    for copy in local[3:]:
        copy.wait()
    m_adj[...] = own_adj[...].reshape(GROUP, SPAN, D)
    gather_second(0, ws_own, ws_oth)
    gather_first(1, wt_own, wt_oth)
    pl.semaphore_wait(plane_sem, 3)
    greet(all_sem, y_line)

    def arrive(n, own, ref):
        @pl.when(stay)
        def _():
            ref[...] = own[...]

        @pl.when(jnp.logical_not(stay))
        def _():
            remote(own, ref, swap_s.at[n], swap_r.at[n], swap_dev).wait()

    arrive(0, own_lat, x_lat)
    swap(1, own_prb, x_prb)
    gather_third(0, ws_oth)
    hid[0] = norm_stats(x_lat[...].astype(F32))[0].astype(BF)

    def project(half, w, slot, q_ref, k_ref, v_ref, q_scale, exchange_rows):
        hidden = hid[slot]
        lanes = pl.ds(0, HALF)
        rows = pl.ds(0, ROWS)
        key = nt(hidden, weight(w, 1))
        k_ref[half, rows, lanes] = key.astype(BF)
        if exchange_rows is not None:
            to_sibling(half, exchange_rows, k_ref).start()
        v_ref[half, rows, lanes] = nt(hidden, weight(w, 2)).astype(BF)
        if exchange_rows is not None:
            to_sibling(half, exchange_rows + 1, v_ref).start()
        q_ref[half, rows, lanes] = nt(hidden, weight(w, 0)).astype(BF)

    def spatial_heads(half, first, last):
        if first == 0:
            mix[half] = jnp.zeros((ROWS, PAD), F32)

        def body(h, carry):
            win, mask = head_window(h)
            k = keep(mask, sk[half, :, win])
            scores = nt(sq[half, :, win], k)
            e = jnp.exp2((scores - jnp.max(scores, axis=-1, keepdims=True)) * EXP2)
            p = e * (1.0 / jnp.sum(e, axis=-1, keepdims=True))
            w = p.astype(BF)
            probs[half * 8 + h] = w
            mix[half, :, win] += nn(w, keep(mask, sv[half, :, win]))
            return carry

        lax.fori_loop(first, last, body, 0, unroll=4)

    def tangent_heads(half, first, last, key_count, q_ref, k_ref, v_ref, dq_ref, dk_ref, dv_ref, p_ref):
        keys = pl.ds(0, key_count)
        if first == 0:
            dmix[half] = jnp.zeros((ROWS, PAD), F32)

        def body(h, carry):
            win, mask = head_window(h)
            k = keep(mask, k_ref[half, keys, win])
            dk = keep(mask, dk_ref[half, keys, win])
            ds = nt(dq_ref[half, :, win], k) + nt(q_ref[half, :, win], dk)
            w = p_ref[half * 8 + h]
            p = w.astype(F32)
            pd = p * (ds * SCALE)
            dp = (pd - p * jnp.sum(pd, axis=-1, keepdims=True)).astype(BF)
            out = nn(dp, keep(mask, v_ref[half, keys, win]))
            out += nn(w, keep(mask, dv_ref[half, keys, win]))
            dmix[half, :, win] += out
            return carry

        lax.fori_loop(first, last, body, 0, unroll=4)

    def out_proj(mixed, w_own, w_oth):
        lanes = pl.ds(0, HALF)
        first = nn(mixed[0, :, lanes].astype(BF), weight(w_own, 3))
        return first + nn(mixed[1, :, lanes].astype(BF), weight(w_oth, 3))

    def siblings(half, pairs):
        for n, ref in pairs:
            to_sibling(half, n, ref).wait()

    primal, moving = ((0, sk), (1, sv)), ((2, sdk), (3, sdv))
    spatial = (2 * ROWS, sq, sk, sv, sdq, sdk, sdv, probs)
    temporal = (ROWS, tq, tk, tv, sdq, sdk, sdv, tprobs)

    project(0, ws_own, 0, sq, sk, sv, None, 0)
    gather_second(1, wt_own, wt_oth)
    siblings(0, primal)
    spatial_heads(0, 0, 8)

    arrive(1, own_prb, x_prb)
    normed, inverse = norm_stats(x_lat[...].astype(F32))
    hid[1] = norm_tangent(normed, inverse, x_prb[...].astype(F32)).astype(BF)
    project(0, ws_own, 1, sdq, sdk, sdv, None, 2)
    gather_fourth(0, ws_oth)
    gather_third(1, wt_oth)
    siblings(0, moving)
    tangent_heads(0, 0, 4, *spatial)
    gather_fifth(0, ws_oth)
    pl.semaphore_wait(all_sem, 7)
    exchange(1, m_adj, r_adj, s, lambda j: (j, t), None)
    tangent_heads(0, 4, 8, *spatial)
    gather_last(0, ws_oth)

    project(1, ws_oth, 0, sq, sk, sv, None, 0)
    project(1, ws_oth, 1, sdq, sdk, sdv, None, 2)
    siblings(1, primal)
    spatial_heads(1, 0, 8)
    inner = (x_lat[...].astype(F32) + out_proj(mix, ws_own, ws_oth)).astype(BF)
    m_inner[...] = inner.reshape(GROUP, SPAN, D)
    exchange(0, m_inner, r_inner, frame, lambda j: (j, c), stay)
    gather_fourth(1, wt_oth)
    siblings(1, moving)
    tangent_heads(1, 0, 8, *spatial)
    gather_fifth(1, wt_oth)
    moved = out_proj(dmix, ws_own, ws_oth)
    tangent = x_prb[...].astype(F32)
    tr_out[...] = jnp.broadcast_to(mean(tangent * moved), (ROWS, 128))
    m_tan[...] = (tangent + moved).astype(BF).reshape(GROUP, SPAN, D)
    exchange(2, m_tan, r_tan, frame, lambda j: (j, c), stay)

    row = lax.broadcasted_iota(jnp.int32, (ROWS, ROWS), 0)
    col = lax.broadcasted_iota(jnp.int32, (ROWS, ROWS), 1)
    same = lax.rem(row, SPAN) == lax.rem(col, SPAN)

    received(0, r_inner)
    x_inner = r_inner[...].reshape(ROWS, D).astype(F32)
    hid[0] = norm_stats(x_inner)[0].astype(BF)
    received(1, r_adj)

    def back_lanes(half, w, g):
        gm = nt(g, weight(w, 3)).astype(BF)
        sdq[half, :, pl.ds(0, HALF)] = gm

    def temporal_heads(half):
        mix[half] = jnp.zeros((ROWS, PAD), F32)
        gq[...] = jnp.zeros(gq.shape, F32)
        gk[...] = jnp.zeros(gk.shape, F32)
        gv[...] = jnp.zeros(gv.shape, F32)

        def body(h, carry):
            win, mask = head_window(h)
            q = tq[half, :, win]
            k = keep(mask, tk[half, :, win])
            v = keep(mask, tv[half, :, win])
            g = sdq[half, :, win]
            scores = jnp.where(same, nt(q, k), -1e30)
            e = jnp.exp2((scores - jnp.max(scores, axis=-1, keepdims=True)) * EXP2)
            p = e * (1.0 / jnp.sum(e, axis=-1, keepdims=True))
            w = p.astype(BF)
            tprobs[half * 8 + h] = w
            mix[half, :, win] += nn(w, v)
            gw = nt(g, v)
            pg = p * (gw * SCALE)
            gs = (pg - p * jnp.sum(pg, axis=-1, keepdims=True)).astype(BF)
            gq[:, win] += nn(gs, k)
            gk[pl.ds(0, ROWS), win] += tn(gs, keep(mask, q))
            gv[pl.ds(0, ROWS), win] += tn(w, keep(mask, g))
            return carry

        lax.fori_loop(0, 8, body, 0, unroll=4)

    def hidden_back(w):
        lanes = pl.ds(0, HALF)
        rows = pl.ds(0, ROWS)
        out = nn(gq[:, lanes].astype(BF), weight(w, 0))
        out += nn(gk[rows, lanes].astype(BF), weight(w, 1))
        return out + nn(gv[rows, lanes].astype(BF), weight(w, 2))

    g_two = r_adj[...].reshape(ROWS, D)
    project(0, wt_own, 0, tq, tk, tv, None, None)
    back_lanes(0, wt_own, g_two)
    temporal_heads(0)
    gh[...] = hidden_back(wt_own)
    gather_last(1, wt_oth)
    project(1, wt_oth, 0, tq, tk, tv, None, None)
    back_lanes(1, wt_oth, r_adj[...].reshape(ROWS, D))
    temporal_heads(1)
    g_hidden = gh[...] + hidden_back(wt_oth)
    normed, inverse = norm_stats(r_inner[...].reshape(ROWS, D).astype(F32))
    grad_two = norm_back(normed, inverse, g_hidden).astype(BF).astype(F32)
    grads_one = (r_adj[...].reshape(ROWS, D).astype(F32) + grad_two).astype(BF)
    m_g[...] = grads_one.reshape(GROUP, SPAN, D)
    exchange(
        3, m_g, r_g, s, lambda f: (lax.div(f, 2) * 2 + t, lax.rem(f, 2)), stay
    )
    reached = r_inner[...].reshape(ROWS, D).astype(F32) + out_proj(mix, wt_own, wt_oth)
    m_u[...] = reached.astype(BF).reshape(GROUP, SPAN, D)

    received(2, r_tan)
    normed, inverse = norm_stats(r_inner[...].reshape(ROWS, D).astype(F32))
    hid[1] = norm_tangent(normed, inverse, r_tan[...].reshape(ROWS, D).astype(F32)).astype(BF)
    project(0, wt_own, 1, sdq, sdk, sdv, None, None)
    project(1, wt_oth, 1, sdq, sdk, sdv, None, None)
    for half in range(2):
        tangent_heads(half, 0, 8, *temporal)
    m_d[...] = out_proj(dmix, wt_own, wt_oth).astype(BF).reshape(GROUP, SPAN, D)

    received(3, r_g)
    exchange(4, m_u, r_u, s, lambda f: (f, t), None)
    exchange(5, m_d, r_d, s, lambda f: (f, t), None)

    def spatial_back(half):
        gq[...] = jnp.zeros(gq.shape, F32)
        gk[...] = jnp.zeros(gk.shape, F32)
        gv[...] = jnp.zeros(gv.shape, F32)

        def body(h, carry):
            win, mask = head_window(h)
            g = sdq[half, :, win]
            w = probs[half * 8 + h]
            p = w.astype(F32)
            gw = nt(g, keep(mask, sv[half, :, win]))
            pg = p * (gw * SCALE)
            gs = (pg - p * jnp.sum(pg, axis=-1, keepdims=True)).astype(BF)
            gq[:, win] += nn(gs, keep(mask, sk[half, :, win]))
            gk[:, win] += tn(gs, keep(mask, sq[half, :, win]))
            gv[:, win] += tn(w, keep(mask, g))
            return carry

        lax.fori_loop(0, 8, body, 0, unroll=4)

    def key_back(half):
        return remote(
            gsib_out.at[half], gsib_in.at[half], gs_s.at[half], gs_r.at[half], sib_dev
        )

    lanes, rows = pl.ds(0, HALF), pl.ds(0, ROWS)
    for half, w in ((0, ws_own), (1, ws_oth)):
        back_lanes(half, w, r_g[...].reshape(ROWS, D))
        spatial_back(half)
        gsib_out[half, 0] = gk[pl.ds(ROWS, ROWS), :].astype(BF)
        gsib_out[half, 1] = gv[pl.ds(ROWS, ROWS), :].astype(BF)
        key_back(half).start()
        if half == 0:
            sq[0] = gq[...].astype(BF)
            sk[0, rows] = gk[rows, :].astype(BF)
            sv[0, rows] = gv[rows, :].astype(BF)
    total = nn(sq[0, :, lanes], weight(ws_own, 0)) + nn(gq[:, lanes].astype(BF), weight(ws_oth, 0))
    key_back(0).wait()
    key = sk[0, rows, lanes].astype(F32) + gsib_in[0, 0, :, lanes].astype(F32)
    value = sv[0, rows, lanes].astype(F32) + gsib_in[0, 1, :, lanes].astype(F32)
    gh[...] = (
        total + nn(key.astype(BF), weight(ws_own, 1)) + nn(value.astype(BF), weight(ws_own, 2))
    )
    key_back(1).wait()

    def to_owner(n):
        piece = pl.ds(n * (ROWS // 2), ROWS // 2)
        return remote(v_out.at[piece], v_in.at[piece], end_s.at[n], end_r.at[n], swap_dev)

    for n in range(2):
        piece = pl.ds(n * (ROWS // 2), ROWS // 2)
        key = gk[piece, lanes] + gsib_in[1, 0, piece, lanes].astype(F32)
        value = gv[piece, lanes] + gsib_in[1, 1, piece, lanes].astype(F32)
        total = gh[piece, :] + nn(key.astype(BF), weight(ws_oth, 1))
        total += nn(value.astype(BF), weight(ws_oth, 2))
        normed, inverse = norm_stats(x_lat[piece, :].astype(F32))
        g_one = r_g[pl.ds(n * (GROUP // 2), GROUP // 2)].reshape(ROWS // 2, D).astype(F32)
        v_out[piece, :] = (norm_back(normed, inverse, total) + g_one).astype(BF)

        @pl.when(jnp.logical_not(stay))
        def _(n=n):
            to_owner(n).start()

    @pl.when(jnp.logical_not(stay))
    def _():
        remote(tr_out, tr_in, end_s.at[2], end_r.at[2], swap_dev).start()

    @pl.when(stay)
    def _():
        v_in[...] = v_out[...]
        tr_in[...] = tr_out[...]

    received(4, r_u)
    o_reached[...] = r_u[...].reshape(ROWS, D)
    received(5, r_d)
    extra = mean(own_prb[...].astype(F32) * r_d[...].reshape(ROWS, D).astype(F32))
    for n, ref, selfless in (
        (0, m_inner, stay), (1, m_adj, None), (2, m_tan, stay),
        (3, m_g, stay), (4, m_u, None), (5, m_d, None),
    ):
        sent(n, ref, selfless)

    @pl.when(jnp.logical_not(stay))
    def _():
        to_owner(0).wait()
        to_owner(1).wait()
        remote(tr_out, tr_in, end_s.at[2], end_r.at[2], swap_dev).wait()

    o_trace[...] = jnp.transpose(tr_in[...] + extra)[0:8]
    o_grads[...] = v_in[...]


def local(latent, probe, adjoint, spatial_qkv, spatial_proj, temporal_qkv, temporal_proj):
    def qkv(w):
        return jnp.transpose(w, (1, 2, 0)).reshape(3, 4, 144, D)

    def proj(w):
        return w.reshape(4, 144, D)

    dma = pltpu.SemaphoreType.DMA
    rows = pltpu.VMEM((ROWS, D), BF)
    weights = pltpu.VMEM((4, 4, 144, D), BF)
    one = pltpu.VMEM((2, ROWS, PAD), BF)
    two = pltpu.VMEM((2, 2 * ROWS, PAD), BF)
    message = pltpu.VMEM((GROUP, SPAN, D), BF)
    scratch = (
        [weights] * 4
        + [rows] * 5
        + [pltpu.VMEM((2, ROWS, D), BF)]
        + [one, two, two, one, two, two]
        + [pltpu.VMEM((16, ROWS, 2 * ROWS), BF)]
        + [one] * 3
        + [pltpu.VMEM((16, ROWS, ROWS), BF)]
        + [pltpu.VMEM((2, ROWS, PAD), F32)] * 2
        + [pltpu.VMEM((ROWS, PAD), F32)]
        + [pltpu.VMEM((2 * ROWS, PAD), F32)] * 2
        + [pltpu.VMEM((2, 2, ROWS, PAD), BF)] * 2
        + [pltpu.VMEM((ROWS, D), F32)]
        + [message] * 12
        + [rows] * 2
        + [pltpu.VMEM((ROWS, 128), F32)] * 2
        + [dma((3,)), dma((4,)), dma((2,)), dma((2,)), dma((2, 4)), dma((2, 4))]
        + [dma((2, 8)), dma((2, 8)), dma((2, 4)), dma((2, 4))]
        + [dma((6,)), dma((6,)), dma((2,)), dma((2,)), dma((3,)), dma((3,))]
        + [pltpu.SemaphoreType.REGULAR] * 2
    )
    reached, grads, trace = pl.pallas_call(
        kernel,
        out_shape=(
            jax.ShapeDtypeStruct((ROWS, D), BF),
            jax.ShapeDtypeStruct((ROWS, D), BF),
            jax.ShapeDtypeStruct((8, ROWS), F32),
        ),
        in_specs=[pl.BlockSpec(memory_space=pl.ANY)] * 7,
        out_specs=[pl.BlockSpec(memory_space=pltpu.VMEM)] * 3,
        scratch_shapes=scratch,
        compiler_params=pltpu.CompilerParams(
            collective_id=0, has_side_effects=True, vmem_limit_bytes=63 << 20
        ),
    )(
        latent, probe, adjoint,
        qkv(spatial_qkv), proj(spatial_proj), qkv(temporal_qkv), proj(temporal_proj),
    )
    new_latent = (0.5 * (latent.astype(F32) + reached[None].astype(F32))).astype(BF)
    new_adjoint = 1.5 * adjoint.astype(F32) - 0.5 * grads[None].astype(F32)
    return new_latent, new_adjoint, trace[0:1]


def solution(mesh):
    in_specs = (
        P("seq", "tp", None),
        P("seq", "tp", None),
        P("seq", "tp", None),
        P(None, None, "tp"),
        P("tp", None),
        P(None, None, "tp"),
        P("tp", None),
    )
    out_specs = (P("seq", "tp", None), P("seq", "tp", None), P("seq", "tp"))
    return jax.shard_map(local, mesh=mesh, in_specs=in_specs, out_specs=out_specs, check_vma=False)
```

```python
import jax
import jax.numpy as jnp
from jax import lax
from jax.experimental import pallas as pl
from jax.experimental.pallas import tpu as pltpu
from jax.sharding import PartitionSpec as P

MESH = pl.DeviceIdType.MESH
BF = jnp.bfloat16
F32 = jnp.float32

epsilon = 1e-06
HEAD = 72
D = 1152
ROWS = 256
HALF = 576
PAD = 640
WIN = 256
GROUP = 64
SPAN = 4
SCALE = HEAD ** (-0.5)
EXP2 = SCALE * 1.4426950408889634


def nt(a, b):
    return lax.dot_general(a, b, (((1,), (1,)), ((), ())), preferred_element_type=F32)


def nn(a, b):
    return lax.dot_general(a, b, (((1,), (0,)), ((), ())), preferred_element_type=F32)


def tn(a, b):
    return lax.dot_general(a, b, (((0,), (0,)), ((), ())), preferred_element_type=F32)


def mean(v):
    return jnp.sum(v, axis=-1, keepdims=True) * (1.0 / D)


def norm_stats(x):
    centred = x - mean(x)
    inverse = lax.rsqrt(mean(centred * centred) + epsilon)
    return centred * inverse, inverse


def norm_tangent(normed, inverse, t):
    centred = t - mean(t)
    return inverse * (centred - normed * mean(normed * centred))


def norm_back(normed, inverse, g):
    return inverse * (g - mean(g) - normed * mean(normed * g))


def weight(ref, kind):
    return ref[kind].reshape(HALF, D)


def head_window(h):
    block = jnp.minimum(lax.div(h * 9, 16), 3)
    base = pl.multiple_of(block * 128, 128)
    lane = lax.broadcasted_iota(jnp.int32, (1, WIN), 1) + block * 128
    return pl.ds(base, WIN), (lane >= h * HEAD) & (lane < h * HEAD + HEAD)


def keep(mask, v):
    return jnp.where(mask, v, jnp.zeros_like(v))


def rank():
    s, t = lax.axis_index("seq"), lax.axis_index("tp")
    return s, t, lax.rem(s, 2)


def kernel(
    latent, probe, adjoint, wsq, wsp, wtq, wtp,
    o_reached, o_grads, o_trace,
    ws_own, ws_oth, wt_own, wt_oth,
    own_lat, own_prb, own_adj, x_lat, x_prb,
    hid, sq, sk, sv, sdq, sdk, sdv, probs,
    tq, tk, tv, tprobs,
    mix, dmix, gq, gk, gv, gsib_out, gsib_in, gh,
    m_inner, m_tan, m_adj, r_inner, r_tan, r_adj,
    m_g, m_u, m_d, r_g, r_u, r_d,
    v_out, v_in, tr_out, tr_in,
    l_sem, w_sem, swap_s, swap_r, sib_s, sib_r,
    gat_s, gat_r, fw_s, fw_r, a2a_s, a2a_r, gs_s, gs_r, end_s, end_r, plane_sem, all_sem,
):
    s, t, c = rank()
    zx = lax.div(s, 4)
    z, x = lax.div(zx, 4), lax.rem(zx, 4)
    low = lax.rem(s, 4)
    stay = c == t
    swap_dev = (s - c + t, c)
    sib_dev = (s + 1 - 2 * c, t)
    y_dev = (s + 2 - 4 * lax.rem(lax.div(s, 2), 2), 1 - t)

    def remote(src, dst, ss, rs, dev):
        return pltpu.make_async_remote_copy(
            src_ref=src, dst_ref=dst, send_sem=ss, recv_sem=rs, device_id=dev, device_id_type=MESH
        )

    local = [
        pltpu.make_async_copy(wsq, ws_own.at[pl.ds(0, 3)], w_sem.at[0]),
        pltpu.make_async_copy(wsp, ws_own.at[3], w_sem.at[1]),
        pltpu.make_async_copy(latent.at[0], own_lat, l_sem.at[0]),
        pltpu.make_async_copy(probe.at[0], own_prb, l_sem.at[1]),
        pltpu.make_async_copy(adjoint.at[0], own_adj, l_sem.at[2]),
        pltpu.make_async_copy(wtq, wt_own.at[pl.ds(0, 3)], w_sem.at[2]),
        pltpu.make_async_copy(wtp, wt_own.at[3], w_sem.at[3]),
    ]
    for copy in local:
        copy.start()
    y_line = [
        (zx * 4 + lax.div(lax.rem(low * 2 + t + k, 8), 2), lax.rem(low * 2 + t + k, 2))
        for k in range(1, 8)
    ]
    x_line = [(z * 16 + lax.rem(x + k, 4) * 4 + low, t) for k in range(1, 4)]
    z_line = [(lax.rem(z + k, 4) * 16 + x * 4 + low, t) for k in range(1, 4)]

    def greet(sem, devices):
        for dev in devices:
            pl.semaphore_signal(sem, inc=1, device_id=dev, device_id_type=MESH)

    barrier = pltpu.get_barrier_semaphore()
    greet(barrier, y_line + x_line + z_line)
    for ref in (sq, sdq, tq):
        ref[:, :, pl.ds(HALF, PAD - HALF)] = jnp.zeros((2, ROWS, PAD - HALF), BF)
    for copy in local[:3]:
        copy.wait()
    pl.semaphore_wait(barrier, 13)

    def parts(emit):
        for core, first, size in ((0, 0, 80), (1, 80, 64)):
            @pl.when(c == core)
            def _(core=core, first=first, size=size):
                emit(core, pl.ds(first, size), size)

    def line(ref, core, i, j, rows):
        if core == 0:
            return ref.at[i, :, rows, :]
        return ref.at[:, j, rows, :]

    def hop(core, k):
        if core == 0:
            return (lax.rem(z + k, 4) * 16 + x * 4 + low, t)
        return (z * 16 + lax.rem(x + k, 4) * 4 + low, t)

    def step(core, k):
        if core == 0:
            return (z * 16 + lax.rem(x + k, 4) * 4 + low, t)
        return (lax.rem(z + k, 4) * 16 + x * 4 + low, t)

    def gather_first(n, own, oth):
        def emit(core, rows, size):
            remote(
                own.at[z, x, rows, :], oth.at[z, x, rows, :],
                gat_s.at[n, 0], gat_r.at[n, 0], y_dev,
            ).start()
        parts(emit)

    def slab(oth, core, a, m, rows):
        if core == 0:
            return oth.at[lax.rem(z - a + 4, 4), lax.rem(x - m + 4, 4), rows, :]
        return oth.at[lax.rem(z - m + 4, 4), lax.rem(x - a + 4, 4), rows, :]

    def push(n, oth, core, a, m, rows, sem, dev):
        block = slab(oth, core, a, m, rows)
        return remote(block, block, gat_s.at[n, sem], gat_r.at[n, sem], dev)

    def pass_on(n, oth, core, m, rows):
        push(n, oth, core, 0, m, rows, 4 + m, hop(core, 1)).start()
        push(n, oth, core, 0, m, rows, 8 + m, hop(core, 3)).start()

    def gather_second(n, own, oth):
        def emit(core, rows, size):
            remote(
                own.at[z, x, rows, :], oth.at[z, x, rows, :],
                gat_s.at[n, 0], gat_r.at[n, 0], y_dev,
            ).wait()
            for k in (1, 3, 2):
                push(n, oth, core, 0, 0, rows, k, step(core, k)).start()
            pass_on(n, oth, core, 0, rows)
        parts(emit)

    def gather_third(n, oth):
        def emit(core, rows, size):
            for k in (1, 3, 2):
                push(n, oth, core, 0, 0, rows, k, step(core, k)).wait_send()
                push(n, oth, core, 0, k, rows, k, step(core, k)).wait_recv()
                pass_on(n, oth, core, k, rows)
            whole = line(oth, core, z, x, rows)
            remote(whole, whole, fw_s.at[n, 0], fw_r.at[n, 0], sib_dev).start()
        parts(emit)

    def gather_fourth(n, oth):
        def emit(core, rows, size):
            for m, sem, a, k in ((0, 4, 1, 1), (1, 5, 1, 1), (3, 11, 3, 3), (2, 10, 3, 3)):
                push(n, oth, core, a, m, rows, sem, hop(core, k)).wait_recv()
                push(n, oth, core, a, m, rows, 12 + m, hop(core, k)).start()
            for m, sem, a in ((3, 7, 1), (2, 6, 1), (0, 8, 3), (1, 9, 3)):
                push(n, oth, core, a, m, rows, sem, hop(core, 1)).wait_recv()
            for a in (1, 3):
                came = line(oth, core, lax.rem(z - a + 4, 4), lax.rem(x - a + 4, 4), rows)
                remote(came, came, fw_s.at[n, a], fw_r.at[n, a], sib_dev).start()
        parts(emit)

    def gather_fifth(n, oth):
        def emit(core, rows, size):
            for m in range(4):
                push(n, oth, core, 2, m, rows, 12 + m, hop(core, 1)).wait_recv()
            came = line(oth, core, lax.rem(z + 2, 4), lax.rem(x + 2, 4), rows)
            remote(came, came, fw_s.at[n, 2], fw_r.at[n, 2], sib_dev).start()
        parts(emit)

    def gather_last(n, oth):
        def emit(core, rows, size):
            whole = line(oth, core, z, x, rows)
            other_rows = pl.ds(80, 64) if core == 0 else pl.ds(0, 80)
            theirs = line(oth, 1 - core, z, x, other_rows)
            for k in range(4):
                remote(theirs, theirs, fw_s.at[n, k], fw_r.at[n, k], sib_dev).wait_recv()
                remote(whole, whole, fw_s.at[n, k], fw_r.at[n, k], sib_dev).wait_send()
            for sem in range(4, 16):
                push(n, oth, core, 0, 0, rows, sem, hop(core, 1)).wait_send()
        parts(emit)

    def exchange(n, src, dst, place, device, selfless):
        def send(k, carry):
            j = lax.rem(s + k, GROUP)
            remote(src.at[j], dst.at[place], a2a_s.at[n], a2a_r.at[n], device(j)).start()
            return carry

        if selfless is None:
            pltpu.make_async_copy(src.at[s], dst.at[s], a2a_r.at[n]).start()
        else:
            @pl.when(selfless)
            def _():
                pltpu.make_async_copy(src.at[s], dst.at[s], a2a_r.at[n]).start()

            @pl.when(jnp.logical_not(selfless))
            def _():
                send(0, 0)
        lax.fori_loop(1, GROUP, send, 0)

    def received(n, dst):
        remote(dst, dst, a2a_s.at[n], a2a_r.at[n], sib_dev).wait_recv()

    def sent(n, src, selfless):
        some = src.at[pl.ds(0, GROUP - 1)]
        remote(some, some, a2a_s.at[n], a2a_r.at[n], sib_dev).wait_send()
        if selfless is not None:
            @pl.when(jnp.logical_not(selfless))
            def _():
                one = src.at[0]
                remote(one, one, a2a_s.at[n], a2a_r.at[n], sib_dev).wait_send()

    def to_sibling(half, n, ref):
        return remote(
            ref.at[half, pl.ds(0, ROWS)], ref.at[half, pl.ds(ROWS, ROWS)],
            sib_s.at[half, n], sib_r.at[half, n], sib_dev,
        )

    frame = s - c + t

    gather_first(0, ws_own, ws_oth)

    def swap(n, own, ref):
        @pl.when(jnp.logical_not(stay))
        def _():
            remote(own, ref, swap_s.at[n], swap_r.at[n], swap_dev).start()

    swap(0, own_lat, x_lat)
    greet(plane_sem, z_line)
    for copy in local[3:]:
        copy.wait()
    m_adj[...] = own_adj[...].reshape(GROUP, SPAN, D)
    gather_second(0, ws_own, ws_oth)
    gather_first(1, wt_own, wt_oth)
    pl.semaphore_wait(plane_sem, 3)
    greet(all_sem, y_line)

    def arrive(n, own, ref):
        @pl.when(stay)
        def _():
            ref[...] = own[...]

        @pl.when(jnp.logical_not(stay))
        def _():
            remote(own, ref, swap_s.at[n], swap_r.at[n], swap_dev).wait()

    arrive(0, own_lat, x_lat)
    swap(1, own_prb, x_prb)
    hid[0] = norm_stats(x_lat[...].astype(F32))[0].astype(BF)

    def project(half, w, slot, q_ref, k_ref, v_ref, q_scale, exchange_rows):
        hidden = hid[slot]
        lanes = pl.ds(0, HALF)
        rows = pl.ds(0, ROWS)
        key = nt(hidden, weight(w, 1))
        k_ref[half, rows, lanes] = key.astype(BF)
        if exchange_rows is not None:
            to_sibling(half, exchange_rows, k_ref).start()
        v_ref[half, rows, lanes] = nt(hidden, weight(w, 2)).astype(BF)
        if exchange_rows is not None:
            to_sibling(half, exchange_rows + 1, v_ref).start()
        q_ref[half, rows, lanes] = nt(hidden, weight(w, 0)).astype(BF)

    def spatial_heads(half, first, last):
        if first == 0:
            mix[half] = jnp.zeros((ROWS, PAD), F32)

        def body(h, carry):
            win, mask = head_window(h)
            k = keep(mask, sk[half, :, win])
            scores = nt(sq[half, :, win], k)
            e = jnp.exp2((scores - jnp.max(scores, axis=-1, keepdims=True)) * EXP2)
            p = e * (1.0 / jnp.sum(e, axis=-1, keepdims=True))
            w = p.astype(BF)
            probs[half * 8 + h] = w
            mix[half, :, win] += nn(w, keep(mask, sv[half, :, win]))
            return carry

        lax.fori_loop(first, last, body, 0, unroll=4)

    def tangent_heads(half, first, last, key_count, q_ref, k_ref, v_ref, dq_ref, dk_ref, dv_ref, p_ref):
        keys = pl.ds(0, key_count)
        if first == 0:
            dmix[half] = jnp.zeros((ROWS, PAD), F32)

        def body(h, carry):
            win, mask = head_window(h)
            k = keep(mask, k_ref[half, keys, win])
            dk = keep(mask, dk_ref[half, keys, win])
            ds = nt(dq_ref[half, :, win], k) + nt(q_ref[half, :, win], dk)
            w = p_ref[half * 8 + h]
            p = w.astype(F32)
            pd = p * (ds * SCALE)
            dp = (pd - p * jnp.sum(pd, axis=-1, keepdims=True)).astype(BF)
            out = nn(dp, keep(mask, v_ref[half, keys, win]))
            out += nn(w, keep(mask, dv_ref[half, keys, win]))
            dmix[half, :, win] += out
            return carry

        lax.fori_loop(first, last, body, 0, unroll=4)

    def out_proj(mixed, w_own, w_oth):
        lanes = pl.ds(0, HALF)
        first = nn(mixed[0, :, lanes].astype(BF), weight(w_own, 3))
        return first + nn(mixed[1, :, lanes].astype(BF), weight(w_oth, 3))

    def siblings(half, pairs):
        for n, ref in pairs:
            to_sibling(half, n, ref).wait()

    primal, moving = ((0, sk), (1, sv)), ((2, sdk), (3, sdv))
    spatial = (2 * ROWS, sq, sk, sv, sdq, sdk, sdv, probs)
    temporal = (ROWS, tq, tk, tv, sdq, sdk, sdv, tprobs)

    project(0, ws_own, 0, sq, sk, sv, None, 0)
    gather_third(0, ws_oth)
    gather_second(1, wt_own, wt_oth)
    siblings(0, primal)
    spatial_heads(0, 0, 8)

    arrive(1, own_prb, x_prb)
    normed, inverse = norm_stats(x_lat[...].astype(F32))
    hid[1] = norm_tangent(normed, inverse, x_prb[...].astype(F32)).astype(BF)
    project(0, ws_own, 1, sdq, sdk, sdv, None, 2)
    gather_fourth(0, ws_oth)
    gather_third(1, wt_oth)
    siblings(0, moving)
    tangent_heads(0, 0, 4, *spatial)
    gather_fifth(0, ws_oth)
    pl.semaphore_wait(all_sem, 7)
    exchange(1, m_adj, r_adj, s, lambda j: (j, t), None)
    tangent_heads(0, 4, 8, *spatial)
    gather_last(0, ws_oth)

    project(1, ws_oth, 0, sq, sk, sv, None, 0)
    project(1, ws_oth, 1, sdq, sdk, sdv, None, 2)
    siblings(1, primal)
    spatial_heads(1, 0, 8)
    inner = (x_lat[...].astype(F32) + out_proj(mix, ws_own, ws_oth)).astype(BF)
    m_inner[...] = inner.reshape(GROUP, SPAN, D)
    exchange(0, m_inner, r_inner, frame, lambda j: (j, c), stay)
    gather_fourth(1, wt_oth)
    siblings(1, moving)
    tangent_heads(1, 0, 8, *spatial)
    gather_fifth(1, wt_oth)
    moved = out_proj(dmix, ws_own, ws_oth)
    tangent = x_prb[...].astype(F32)
    tr_out[...] = jnp.broadcast_to(mean(tangent * moved), (ROWS, 128))
    m_tan[...] = (tangent + moved).astype(BF).reshape(GROUP, SPAN, D)
    exchange(2, m_tan, r_tan, frame, lambda j: (j, c), stay)

    row = lax.broadcasted_iota(jnp.int32, (ROWS, ROWS), 0)
    col = lax.broadcasted_iota(jnp.int32, (ROWS, ROWS), 1)
    same = lax.rem(row, SPAN) == lax.rem(col, SPAN)

    received(0, r_inner)
    x_inner = r_inner[...].reshape(ROWS, D).astype(F32)
    hid[0] = norm_stats(x_inner)[0].astype(BF)
    received(1, r_adj)

    def back_lanes(half, w, g):
        gm = nt(g, weight(w, 3)).astype(BF)
        sdq[half, :, pl.ds(0, HALF)] = gm

    def temporal_heads(half):
        mix[half] = jnp.zeros((ROWS, PAD), F32)
        gq[...] = jnp.zeros(gq.shape, F32)
        gk[...] = jnp.zeros(gk.shape, F32)
        gv[...] = jnp.zeros(gv.shape, F32)

        def body(h, carry):
            win, mask = head_window(h)
            q = tq[half, :, win]
            k = keep(mask, tk[half, :, win])
            v = keep(mask, tv[half, :, win])
            g = sdq[half, :, win]
            scores = jnp.where(same, nt(q, k), -1e30)
            e = jnp.exp2((scores - jnp.max(scores, axis=-1, keepdims=True)) * EXP2)
            p = e * (1.0 / jnp.sum(e, axis=-1, keepdims=True))
            w = p.astype(BF)
            tprobs[half * 8 + h] = w
            mix[half, :, win] += nn(w, v)
            gw = nt(g, v)
            pg = p * (gw * SCALE)
            gs = (pg - p * jnp.sum(pg, axis=-1, keepdims=True)).astype(BF)
            gq[:, win] += nn(gs, k)
            gk[pl.ds(0, ROWS), win] += tn(gs, keep(mask, q))
            gv[pl.ds(0, ROWS), win] += tn(w, keep(mask, g))
            return carry

        lax.fori_loop(0, 8, body, 0, unroll=4)

    def hidden_back(w):
        lanes = pl.ds(0, HALF)
        rows = pl.ds(0, ROWS)
        out = nn(gq[:, lanes].astype(BF), weight(w, 0))
        out += nn(gk[rows, lanes].astype(BF), weight(w, 1))
        return out + nn(gv[rows, lanes].astype(BF), weight(w, 2))

    g_two = r_adj[...].reshape(ROWS, D)
    project(0, wt_own, 0, tq, tk, tv, None, None)
    back_lanes(0, wt_own, g_two)
    temporal_heads(0)
    gh[...] = hidden_back(wt_own)
    gather_last(1, wt_oth)
    project(1, wt_oth, 0, tq, tk, tv, None, None)
    back_lanes(1, wt_oth, r_adj[...].reshape(ROWS, D))
    temporal_heads(1)
    g_hidden = gh[...] + hidden_back(wt_oth)
    normed, inverse = norm_stats(r_inner[...].reshape(ROWS, D).astype(F32))
    grad_two = norm_back(normed, inverse, g_hidden).astype(BF).astype(F32)
    grads_one = (r_adj[...].reshape(ROWS, D).astype(F32) + grad_two).astype(BF)
    m_g[...] = grads_one.reshape(GROUP, SPAN, D)
    exchange(
        3, m_g, r_g, s, lambda f: (lax.div(f, 2) * 2 + t, lax.rem(f, 2)), stay
    )
    reached = r_inner[...].reshape(ROWS, D).astype(F32) + out_proj(mix, wt_own, wt_oth)
    m_u[...] = reached.astype(BF).reshape(GROUP, SPAN, D)

    received(2, r_tan)
    normed, inverse = norm_stats(r_inner[...].reshape(ROWS, D).astype(F32))
    hid[1] = norm_tangent(normed, inverse, r_tan[...].reshape(ROWS, D).astype(F32)).astype(BF)
    project(0, wt_own, 1, sdq, sdk, sdv, None, None)
    project(1, wt_oth, 1, sdq, sdk, sdv, None, None)
    for half in range(2):
        tangent_heads(half, 0, 8, *temporal)
    m_d[...] = out_proj(dmix, wt_own, wt_oth).astype(BF).reshape(GROUP, SPAN, D)

    received(3, r_g)
    exchange(4, m_u, r_u, s, lambda f: (f, t), None)
    exchange(5, m_d, r_d, s, lambda f: (f, t), None)

    def spatial_back(half):
        gq[...] = jnp.zeros(gq.shape, F32)
        gk[...] = jnp.zeros(gk.shape, F32)
        gv[...] = jnp.zeros(gv.shape, F32)

        def body(h, carry):
            win, mask = head_window(h)
            g = sdq[half, :, win]
            w = probs[half * 8 + h]
            p = w.astype(F32)
            gw = nt(g, keep(mask, sv[half, :, win]))
            pg = p * (gw * SCALE)
            gs = (pg - p * jnp.sum(pg, axis=-1, keepdims=True)).astype(BF)
            gq[:, win] += nn(gs, keep(mask, sk[half, :, win]))
            gk[:, win] += tn(gs, keep(mask, sq[half, :, win]))
            gv[:, win] += tn(w, keep(mask, g))
            return carry

        lax.fori_loop(0, 8, body, 0, unroll=4)

    def key_back(half):
        return remote(
            gsib_out.at[half], gsib_in.at[half], gs_s.at[half], gs_r.at[half], sib_dev
        )

    lanes, rows = pl.ds(0, HALF), pl.ds(0, ROWS)
    for half, w in ((0, ws_own), (1, ws_oth)):
        back_lanes(half, w, r_g[...].reshape(ROWS, D))
        spatial_back(half)
        gsib_out[half, 0] = gk[pl.ds(ROWS, ROWS), :].astype(BF)
        gsib_out[half, 1] = gv[pl.ds(ROWS, ROWS), :].astype(BF)
        key_back(half).start()
        if half == 0:
            sq[0] = gq[...].astype(BF)
            sk[0, rows] = gk[rows, :].astype(BF)
            sv[0, rows] = gv[rows, :].astype(BF)
    total = nn(sq[0, :, lanes], weight(ws_own, 0)) + nn(gq[:, lanes].astype(BF), weight(ws_oth, 0))
    key_back(0).wait()
    key = sk[0, rows, lanes].astype(F32) + gsib_in[0, 0, :, lanes].astype(F32)
    value = sv[0, rows, lanes].astype(F32) + gsib_in[0, 1, :, lanes].astype(F32)
    gh[...] = (
        total + nn(key.astype(BF), weight(ws_own, 1)) + nn(value.astype(BF), weight(ws_own, 2))
    )
    key_back(1).wait()

    def to_owner(n):
        piece = pl.ds(n * (ROWS // 2), ROWS // 2)
        return remote(v_out.at[piece], v_in.at[piece], end_s.at[n], end_r.at[n], swap_dev)

    for n in range(2):
        piece = pl.ds(n * (ROWS // 2), ROWS // 2)
        key = gk[piece, lanes] + gsib_in[1, 0, piece, lanes].astype(F32)
        value = gv[piece, lanes] + gsib_in[1, 1, piece, lanes].astype(F32)
        total = gh[piece, :] + nn(key.astype(BF), weight(ws_oth, 1))
        total += nn(value.astype(BF), weight(ws_oth, 2))
        normed, inverse = norm_stats(x_lat[piece, :].astype(F32))
        g_one = r_g[pl.ds(n * (GROUP // 2), GROUP // 2)].reshape(ROWS // 2, D).astype(F32)
        v_out[piece, :] = (norm_back(normed, inverse, total) + g_one).astype(BF)

        @pl.when(jnp.logical_not(stay))
        def _(n=n):
            to_owner(n).start()

    @pl.when(jnp.logical_not(stay))
    def _():
        remote(tr_out, tr_in, end_s.at[2], end_r.at[2], swap_dev).start()

    @pl.when(stay)
    def _():
        v_in[...] = v_out[...]
        tr_in[...] = tr_out[...]

    received(4, r_u)
    o_reached[...] = r_u[...].reshape(ROWS, D)
    received(5, r_d)
    extra = mean(own_prb[...].astype(F32) * r_d[...].reshape(ROWS, D).astype(F32))
    for n, ref, selfless in (
        (0, m_inner, stay), (1, m_adj, None), (2, m_tan, stay),
        (3, m_g, stay), (4, m_u, None), (5, m_d, None),
    ):
        sent(n, ref, selfless)

    @pl.when(jnp.logical_not(stay))
    def _():
        to_owner(0).wait()
        to_owner(1).wait()
        remote(tr_out, tr_in, end_s.at[2], end_r.at[2], swap_dev).wait()

    o_trace[...] = jnp.transpose(tr_in[...] + extra)[0:8]
    o_grads[...] = v_in[...]


def local(latent, probe, adjoint, spatial_qkv, spatial_proj, temporal_qkv, temporal_proj):
    def qkv(w):
        return jnp.transpose(w, (1, 2, 0)).reshape(3, 4, 144, D)

    def proj(w):
        return w.reshape(4, 144, D)

    dma = pltpu.SemaphoreType.DMA
    rows = pltpu.VMEM((ROWS, D), BF)
    weights = pltpu.VMEM((4, 4, 144, D), BF)
    one = pltpu.VMEM((2, ROWS, PAD), BF)
    two = pltpu.VMEM((2, 2 * ROWS, PAD), BF)
    message = pltpu.VMEM((GROUP, SPAN, D), BF)
    scratch = (
        [weights] * 4
        + [rows] * 5
        + [pltpu.VMEM((2, ROWS, D), BF)]
        + [one, two, two, one, two, two]
        + [pltpu.VMEM((16, ROWS, 2 * ROWS), BF)]
        + [one] * 3
        + [pltpu.VMEM((16, ROWS, ROWS), BF)]
        + [pltpu.VMEM((2, ROWS, PAD), F32)] * 2
        + [pltpu.VMEM((ROWS, PAD), F32)]
        + [pltpu.VMEM((2 * ROWS, PAD), F32)] * 2
        + [pltpu.VMEM((2, 2, ROWS, PAD), BF)] * 2
        + [pltpu.VMEM((ROWS, D), F32)]
        + [message] * 12
        + [rows] * 2
        + [pltpu.VMEM((ROWS, 128), F32)] * 2
        + [dma((3,)), dma((4,)), dma((2,)), dma((2,)), dma((2, 4)), dma((2, 4))]
        + [dma((2, 16)), dma((2, 16)), dma((2, 4)), dma((2, 4))]
        + [dma((6,)), dma((6,)), dma((2,)), dma((2,)), dma((3,)), dma((3,))]
        + [pltpu.SemaphoreType.REGULAR] * 2
    )
    reached, grads, trace = pl.pallas_call(
        kernel,
        out_shape=(
            jax.ShapeDtypeStruct((ROWS, D), BF),
            jax.ShapeDtypeStruct((ROWS, D), BF),
            jax.ShapeDtypeStruct((8, ROWS), F32),
        ),
        in_specs=[pl.BlockSpec(memory_space=pl.ANY)] * 7,
        out_specs=[pl.BlockSpec(memory_space=pltpu.VMEM)] * 3,
        scratch_shapes=scratch,
        compiler_params=pltpu.CompilerParams(
            collective_id=0, has_side_effects=True, vmem_limit_bytes=63 << 20
        ),
    )(
        latent, probe, adjoint,
        qkv(spatial_qkv), proj(spatial_proj), qkv(temporal_qkv), proj(temporal_proj),
    )
    new_latent = (0.5 * (latent.astype(F32) + reached[None].astype(F32))).astype(BF)
    new_adjoint = 1.5 * adjoint.astype(F32) - 0.5 * grads[None].astype(F32)
    return new_latent, new_adjoint, trace[0:1]


def solution(mesh):
    in_specs = (
        P("seq", "tp", None),
        P("seq", "tp", None),
        P("seq", "tp", None),
        P(None, None, "tp"),
        P("tp", None),
        P(None, None, "tp"),
        P("tp", None),
    )
    out_specs = (P("seq", "tp", None), P("seq", "tp", None), P("seq", "tp"))
    return jax.shard_map(local, mesh=mesh, in_specs=in_specs, out_specs=out_specs, check_vma=False)
```

```python
import jax
import jax.numpy as jnp
from jax import lax
from jax.experimental import pallas as pl
from jax.experimental.pallas import tpu as pltpu
from jax.sharding import PartitionSpec as P

MESH = pl.DeviceIdType.MESH
BF = jnp.bfloat16
F32 = jnp.float32

epsilon = 1e-06
HEAD = 72
D = 1152
ROWS = 256
HALF = 576
PAD = 640
WIN = 256
GROUP = 64
SPAN = 4
SCALE = HEAD ** (-0.5)
EXP2 = SCALE * 1.4426950408889634


def nt(a, b):
    return lax.dot_general(a, b, (((1,), (1,)), ((), ())), preferred_element_type=F32)


def nn(a, b):
    return lax.dot_general(a, b, (((1,), (0,)), ((), ())), preferred_element_type=F32)


def tn(a, b):
    return lax.dot_general(a, b, (((0,), (0,)), ((), ())), preferred_element_type=F32)


def mean(v):
    return jnp.sum(v, axis=-1, keepdims=True) * (1.0 / D)


def norm_stats(x):
    centred = x - mean(x)
    inverse = lax.rsqrt(mean(centred * centred) + epsilon)
    return centred * inverse, inverse


def norm_tangent(normed, inverse, t):
    centred = t - mean(t)
    return inverse * (centred - normed * mean(normed * centred))


def norm_back(normed, inverse, g):
    return inverse * (g - mean(g) - normed * mean(normed * g))


def weight(ref, kind):
    return ref[kind].reshape(HALF, D)


def head_window(h):
    block = jnp.minimum(lax.div(h * 9, 16), 3)
    base = pl.multiple_of(block * 128, 128)
    lane = lax.broadcasted_iota(jnp.int32, (1, WIN), 1) + block * 128
    return pl.ds(base, WIN), (lane >= h * HEAD) & (lane < h * HEAD + HEAD)


def keep(mask, v):
    return jnp.where(mask, v, jnp.zeros_like(v))


def rank():
    s, t = lax.axis_index("seq"), lax.axis_index("tp")
    return s, t, lax.rem(s, 2)


def kernel(
    latent, probe, adjoint, wsq, wsp, wtq, wtp,
    o_reached, o_grads, o_trace,
    ws_own, ws_oth, wt_own, wt_oth,
    own_lat, own_prb, own_adj, x_lat, x_prb,
    hid, sq, sk, sv, sdq, sdk, sdv, probs,
    tq, tk, tv, tprobs,
    mix, dmix, gq, gk, gv, gsib_out, gsib_in, gh,
    m_inner, m_tan, m_adj, r_inner, r_tan, r_adj,
    m_g, m_u, m_d, r_g, r_u, r_d,
    v_out, v_in, tr_out, tr_in,
    l_sem, w_sem, swap_s, swap_r, sib_s, sib_r,
    gat_s, gat_r, fw_s, fw_r, a2a_s, a2a_r, gs_s, gs_r, end_s, end_r, plane_sem, all_sem,
):
    s, t, c = rank()
    zx = lax.div(s, 4)
    z, x = lax.div(zx, 4), lax.rem(zx, 4)
    low = lax.rem(s, 4)
    stay = c == t
    swap_dev = (s - c + t, c)
    sib_dev = (s + 1 - 2 * c, t)
    y_dev = (s + 2 - 4 * lax.rem(lax.div(s, 2), 2), 1 - t)

    def remote(src, dst, ss, rs, dev):
        return pltpu.make_async_remote_copy(
            src_ref=src, dst_ref=dst, send_sem=ss, recv_sem=rs, device_id=dev, device_id_type=MESH
        )

    local = [
        pltpu.make_async_copy(wsq, ws_own.at[pl.ds(0, 3)], w_sem.at[0]),
        pltpu.make_async_copy(wsp, ws_own.at[3], w_sem.at[1]),
        pltpu.make_async_copy(latent.at[0], own_lat, l_sem.at[0]),
        pltpu.make_async_copy(probe.at[0], own_prb, l_sem.at[1]),
        pltpu.make_async_copy(adjoint.at[0], own_adj, l_sem.at[2]),
        pltpu.make_async_copy(wtq, wt_own.at[pl.ds(0, 3)], w_sem.at[2]),
        pltpu.make_async_copy(wtp, wt_own.at[3], w_sem.at[3]),
    ]
    for copy in local:
        copy.start()
    y_line = [
        (zx * 4 + lax.div(lax.rem(low * 2 + t + k, 8), 2), lax.rem(low * 2 + t + k, 2))
        for k in range(1, 8)
    ]
    x_line = [(z * 16 + lax.rem(x + k, 4) * 4 + low, t) for k in range(1, 4)]
    z_line = [(lax.rem(z + k, 4) * 16 + x * 4 + low, t) for k in range(1, 4)]

    def greet(sem, devices):
        for dev in devices:
            pl.semaphore_signal(sem, inc=1, device_id=dev, device_id_type=MESH)

    barrier = pltpu.get_barrier_semaphore()
    greet(barrier, y_line + x_line + z_line)
    for ref in (sq, sdq, tq):
        ref[:, :, pl.ds(HALF, PAD - HALF)] = jnp.zeros((2, ROWS, PAD - HALF), BF)
    for copy in local[:3]:
        copy.wait()
    pl.semaphore_wait(barrier, 13)

    def parts(emit):
        for core, first, size in ((0, 0, 80), (1, 80, 64)):
            @pl.when(c == core)
            def _(core=core, first=first, size=size):
                emit(core, pl.ds(first, size), size)

    def line(ref, core, i, j, rows):
        if core == 0:
            return ref.at[i, :, rows, :]
        return ref.at[:, j, rows, :]

    def hop(core, k):
        if core == 0:
            return (lax.rem(z + k, 4) * 16 + x * 4 + low, t)
        return (z * 16 + lax.rem(x + k, 4) * 4 + low, t)

    def step(core, k):
        if core == 0:
            return (z * 16 + lax.rem(x + k, 4) * 4 + low, t)
        return (lax.rem(z + k, 4) * 16 + x * 4 + low, t)

    def gather_first(n, own, oth):
        def emit(core, rows, size):
            remote(
                own.at[z, x, rows, :], oth.at[z, x, rows, :],
                gat_s.at[n, 0], gat_r.at[n, 0], y_dev,
            ).start()
        parts(emit)

    def slab(oth, core, a, m, rows):
        if core == 0:
            return oth.at[lax.rem(z - a + 4, 4), lax.rem(x - m + 4, 4), rows, :]
        return oth.at[lax.rem(z - m + 4, 4), lax.rem(x - a + 4, 4), rows, :]

    def push(n, oth, core, a, m, rows, sem, dev):
        block = slab(oth, core, a, m, rows)
        return remote(block, block, gat_s.at[n, sem], gat_r.at[n, sem], dev)

    def pass_on(n, oth, core, m, rows):
        push(n, oth, core, 0, m, rows, 4 + m, hop(core, 1)).start()
        push(n, oth, core, 0, m, rows, 8 + m, hop(core, 3)).start()

    def gather_second(n, own, oth):
        def emit(core, rows, size):
            remote(
                own.at[z, x, rows, :], oth.at[z, x, rows, :],
                gat_s.at[n, 0], gat_r.at[n, 0], y_dev,
            ).wait()
            for k in (1, 3, 2):
                push(n, oth, core, 0, 0, rows, k, step(core, k)).start()
            pass_on(n, oth, core, 0, rows)
        parts(emit)

    def gather_third(n, oth):
        def emit(core, rows, size):
            for k in (1, 3, 2):
                push(n, oth, core, 0, 0, rows, k, step(core, k)).wait_send()
                push(n, oth, core, 0, k, rows, k, step(core, k)).wait_recv()
                pass_on(n, oth, core, k, rows)
            whole = line(oth, core, z, x, rows)
            remote(whole, whole, fw_s.at[n, 0], fw_r.at[n, 0], sib_dev).start()
        parts(emit)

    def gather_fourth(n, oth):
        def emit(core, rows, size):
            for m, sem, a, k in ((0, 4, 1, 1), (1, 5, 1, 1), (3, 11, 3, 3), (2, 10, 3, 3)):
                push(n, oth, core, a, m, rows, sem, hop(core, k)).wait_recv()
                push(n, oth, core, a, m, rows, 12 + m, hop(core, k)).start()
            for m, sem, a in ((3, 7, 1), (2, 6, 1), (0, 8, 3), (1, 9, 3)):
                push(n, oth, core, a, m, rows, sem, hop(core, 1)).wait_recv()
            for a in (1, 3):
                came = line(oth, core, lax.rem(z - a + 4, 4), lax.rem(x - a + 4, 4), rows)
                remote(came, came, fw_s.at[n, a], fw_r.at[n, a], sib_dev).start()
        parts(emit)

    def gather_fifth(n, oth):
        def emit(core, rows, size):
            for m in range(4):
                push(n, oth, core, 2, m, rows, 12 + m, hop(core, 1)).wait_recv()
            came = line(oth, core, lax.rem(z + 2, 4), lax.rem(x + 2, 4), rows)
            remote(came, came, fw_s.at[n, 2], fw_r.at[n, 2], sib_dev).start()
        parts(emit)

    def gather_last(n, oth):
        def emit(core, rows, size):
            whole = line(oth, core, z, x, rows)
            other_rows = pl.ds(80, 64) if core == 0 else pl.ds(0, 80)
            theirs = line(oth, 1 - core, z, x, other_rows)
            for k in range(4):
                remote(theirs, theirs, fw_s.at[n, k], fw_r.at[n, k], sib_dev).wait_recv()
                remote(whole, whole, fw_s.at[n, k], fw_r.at[n, k], sib_dev).wait_send()
            for sem in range(4, 16):
                push(n, oth, core, 0, 0, rows, sem, hop(core, 1)).wait_send()
        parts(emit)

    def exchange(n, src, dst, place, device, selfless):
        def send(k, carry):
            j = lax.rem(s + k, GROUP)
            remote(src.at[j], dst.at[place], a2a_s.at[n], a2a_r.at[n], device(j)).start()
            return carry

        if selfless is None:
            pltpu.make_async_copy(src.at[s], dst.at[s], a2a_r.at[n]).start()
        else:
            @pl.when(selfless)
            def _():
                pltpu.make_async_copy(src.at[s], dst.at[s], a2a_r.at[n]).start()

            @pl.when(jnp.logical_not(selfless))
            def _():
                send(0, 0)
        lax.fori_loop(1, GROUP, send, 0)

    def received(n, dst):
        remote(dst, dst, a2a_s.at[n], a2a_r.at[n], sib_dev).wait_recv()

    def sent(n, src, selfless):
        some = src.at[pl.ds(0, GROUP - 1)]
        remote(some, some, a2a_s.at[n], a2a_r.at[n], sib_dev).wait_send()
        if selfless is not None:
            @pl.when(jnp.logical_not(selfless))
            def _():
                one = src.at[0]
                remote(one, one, a2a_s.at[n], a2a_r.at[n], sib_dev).wait_send()

    def to_sibling(half, n, ref):
        return remote(
            ref.at[half, pl.ds(0, ROWS)], ref.at[half, pl.ds(ROWS, ROWS)],
            sib_s.at[half, n], sib_r.at[half, n], sib_dev,
        )

    frame = s - c + t

    gather_first(0, ws_own, ws_oth)

    def swap(n, own, ref):
        @pl.when(jnp.logical_not(stay))
        def _():
            remote(own, ref, swap_s.at[n], swap_r.at[n], swap_dev).start()

    swap(0, own_lat, x_lat)
    greet(plane_sem, z_line)
    for copy in local[3:]:
        copy.wait()
    m_adj[...] = own_adj[...].reshape(GROUP, SPAN, D)
    gather_second(0, ws_own, ws_oth)
    gather_first(1, wt_own, wt_oth)
    pl.semaphore_wait(plane_sem, 3)
    greet(all_sem, y_line)

    def arrive(n, own, ref):
        @pl.when(stay)
        def _():
            ref[...] = own[...]

        @pl.when(jnp.logical_not(stay))
        def _():
            remote(own, ref, swap_s.at[n], swap_r.at[n], swap_dev).wait()

    arrive(0, own_lat, x_lat)
    swap(1, own_prb, x_prb)
    hid[0] = norm_stats(x_lat[...].astype(F32))[0].astype(BF)

    def project(half, w, slot, q_ref, k_ref, v_ref, q_scale, exchange_rows):
        hidden = hid[slot]
        lanes = pl.ds(0, HALF)
        rows = pl.ds(0, ROWS)
        key = nt(hidden, weight(w, 1))
        k_ref[half, rows, lanes] = key.astype(BF)
        if exchange_rows is not None:
            to_sibling(half, exchange_rows, k_ref).start()
        v_ref[half, rows, lanes] = nt(hidden, weight(w, 2)).astype(BF)
        if exchange_rows is not None:
            to_sibling(half, exchange_rows + 1, v_ref).start()
        q_ref[half, rows, lanes] = nt(hidden, weight(w, 0)).astype(BF)

    def spatial_heads(half, first, last):
        if first == 0:
            mix[half] = jnp.zeros((ROWS, PAD), F32)

        def body(h, carry):
            win, mask = head_window(h)
            k = keep(mask, sk[half, :, win])
            scores = nt(sq[half, :, win], k)
            e = jnp.exp2((scores - jnp.max(scores, axis=-1, keepdims=True)) * EXP2)
            p = e * (1.0 / jnp.sum(e, axis=-1, keepdims=True))
            w = p.astype(BF)
            probs[half * 8 + h] = w
            mix[half, :, win] += nn(w, keep(mask, sv[half, :, win]))
            return carry

        lax.fori_loop(first, last, body, 0, unroll=4)

    def tangent_heads(half, first, last, key_count, q_ref, k_ref, v_ref, dq_ref, dk_ref, dv_ref, p_ref):
        keys = pl.ds(0, key_count)
        if first == 0:
            dmix[half] = jnp.zeros((ROWS, PAD), F32)

        def body(h, carry):
            win, mask = head_window(h)
            k = keep(mask, k_ref[half, keys, win])
            dk = keep(mask, dk_ref[half, keys, win])
            ds = nt(dq_ref[half, :, win], k) + nt(q_ref[half, :, win], dk)
            w = p_ref[half * 8 + h]
            p = w.astype(F32)
            pd = p * (ds * SCALE)
            dp = (pd - p * jnp.sum(pd, axis=-1, keepdims=True)).astype(BF)
            out = nn(dp, keep(mask, v_ref[half, keys, win]))
            out += nn(w, keep(mask, dv_ref[half, keys, win]))
            dmix[half, :, win] += out
            return carry

        lax.fori_loop(first, last, body, 0, unroll=4)

    def out_proj(mixed, w_own, w_oth):
        lanes = pl.ds(0, HALF)
        first = nn(mixed[0, :, lanes].astype(BF), weight(w_own, 3))
        return first + nn(mixed[1, :, lanes].astype(BF), weight(w_oth, 3))

    def siblings(half, pairs):
        for n, ref in pairs:
            to_sibling(half, n, ref).wait()

    primal, moving = ((0, sk), (1, sv)), ((2, sdk), (3, sdv))
    spatial = (2 * ROWS, sq, sk, sv, sdq, sdk, sdv, probs)
    temporal = (ROWS, tq, tk, tv, sdq, sdk, sdv, tprobs)

    project(0, ws_own, 0, sq, sk, sv, None, 0)
    gather_third(0, ws_oth)
    gather_second(1, wt_own, wt_oth)
    siblings(0, primal)
    spatial_heads(0, 0, 8)

    arrive(1, own_prb, x_prb)
    normed, inverse = norm_stats(x_lat[...].astype(F32))
    hid[1] = norm_tangent(normed, inverse, x_prb[...].astype(F32)).astype(BF)
    project(0, ws_own, 1, sdq, sdk, sdv, None, 2)
    gather_third(1, wt_oth)
    gather_fourth(0, ws_oth)
    siblings(0, moving)
    tangent_heads(0, 0, 4, *spatial)
    gather_fifth(0, ws_oth)
    pl.semaphore_wait(all_sem, 7)
    exchange(1, m_adj, r_adj, s, lambda j: (j, t), None)
    tangent_heads(0, 4, 8, *spatial)
    gather_last(0, ws_oth)

    project(1, ws_oth, 0, sq, sk, sv, None, 0)
    project(1, ws_oth, 1, sdq, sdk, sdv, None, 2)
    siblings(1, primal)
    spatial_heads(1, 0, 8)
    inner = (x_lat[...].astype(F32) + out_proj(mix, ws_own, ws_oth)).astype(BF)
    m_inner[...] = inner.reshape(GROUP, SPAN, D)
    exchange(0, m_inner, r_inner, frame, lambda j: (j, c), stay)
    gather_fourth(1, wt_oth)
    siblings(1, moving)
    tangent_heads(1, 0, 8, *spatial)
    gather_fifth(1, wt_oth)
    moved = out_proj(dmix, ws_own, ws_oth)
    tangent = x_prb[...].astype(F32)
    tr_out[...] = jnp.broadcast_to(mean(tangent * moved), (ROWS, 128))
    m_tan[...] = (tangent + moved).astype(BF).reshape(GROUP, SPAN, D)
    exchange(2, m_tan, r_tan, frame, lambda j: (j, c), stay)

    row = lax.broadcasted_iota(jnp.int32, (ROWS, ROWS), 0)
    col = lax.broadcasted_iota(jnp.int32, (ROWS, ROWS), 1)
    same = lax.rem(row, SPAN) == lax.rem(col, SPAN)

    def back_lanes(half, w, g):
        gm = nt(g, weight(w, 3)).astype(BF)
        sdq[half, :, pl.ds(0, HALF)] = gm

    received(1, r_adj)
    back_lanes(0, wt_own, r_adj[...].reshape(ROWS, D))
    received(0, r_inner)
    x_inner = r_inner[...].reshape(ROWS, D).astype(F32)
    hid[0] = norm_stats(x_inner)[0].astype(BF)

    def temporal_heads(half):
        mix[half] = jnp.zeros((ROWS, PAD), F32)
        gq[...] = jnp.zeros(gq.shape, F32)
        gk[...] = jnp.zeros(gk.shape, F32)
        gv[...] = jnp.zeros(gv.shape, F32)

        def body(h, carry):
            win, mask = head_window(h)
            q = tq[half, :, win]
            k = keep(mask, tk[half, :, win])
            v = keep(mask, tv[half, :, win])
            g = sdq[half, :, win]
            scores = jnp.where(same, nt(q, k), -1e30)
            e = jnp.exp2((scores - jnp.max(scores, axis=-1, keepdims=True)) * EXP2)
            p = e * (1.0 / jnp.sum(e, axis=-1, keepdims=True))
            w = p.astype(BF)
            tprobs[half * 8 + h] = w
            mix[half, :, win] += nn(w, v)
            gw = nt(g, v)
            pg = p * (gw * SCALE)
            gs = (pg - p * jnp.sum(pg, axis=-1, keepdims=True)).astype(BF)
            gq[:, win] += nn(gs, k)
            gk[pl.ds(0, ROWS), win] += tn(gs, keep(mask, q))
            gv[pl.ds(0, ROWS), win] += tn(w, keep(mask, g))
            return carry

        lax.fori_loop(0, 8, body, 0, unroll=4)

    def hidden_back(w):
        lanes = pl.ds(0, HALF)
        rows = pl.ds(0, ROWS)
        out = nn(gq[:, lanes].astype(BF), weight(w, 0))
        out += nn(gk[rows, lanes].astype(BF), weight(w, 1))
        return out + nn(gv[rows, lanes].astype(BF), weight(w, 2))

    project(0, wt_own, 0, tq, tk, tv, None, None)
    temporal_heads(0)
    gh[...] = hidden_back(wt_own)
    gather_last(1, wt_oth)
    project(1, wt_oth, 0, tq, tk, tv, None, None)
    back_lanes(1, wt_oth, r_adj[...].reshape(ROWS, D))
    temporal_heads(1)
    g_hidden = gh[...] + hidden_back(wt_oth)
    normed, inverse = norm_stats(r_inner[...].reshape(ROWS, D).astype(F32))
    grad_two = norm_back(normed, inverse, g_hidden).astype(BF).astype(F32)
    grads_one = (r_adj[...].reshape(ROWS, D).astype(F32) + grad_two).astype(BF)
    m_g[...] = grads_one.reshape(GROUP, SPAN, D)
    exchange(
        3, m_g, r_g, s, lambda f: (lax.div(f, 2) * 2 + t, lax.rem(f, 2)), stay
    )
    reached = r_inner[...].reshape(ROWS, D).astype(F32) + out_proj(mix, wt_own, wt_oth)
    m_u[...] = reached.astype(BF).reshape(GROUP, SPAN, D)

    received(2, r_tan)
    normed, inverse = norm_stats(r_inner[...].reshape(ROWS, D).astype(F32))
    hid[1] = norm_tangent(normed, inverse, r_tan[...].reshape(ROWS, D).astype(F32)).astype(BF)
    project(0, wt_own, 1, sdq, sdk, sdv, None, None)
    project(1, wt_oth, 1, sdq, sdk, sdv, None, None)
    for half in range(2):
        tangent_heads(half, 0, 8, *temporal)
    m_d[...] = out_proj(dmix, wt_own, wt_oth).astype(BF).reshape(GROUP, SPAN, D)

    received(3, r_g)
    exchange(4, m_u, r_u, s, lambda f: (f, t), None)
    exchange(5, m_d, r_d, s, lambda f: (f, t), None)

    def spatial_back(half):
        gq[...] = jnp.zeros(gq.shape, F32)
        gk[...] = jnp.zeros(gk.shape, F32)
        gv[...] = jnp.zeros(gv.shape, F32)

        def body(h, carry):
            win, mask = head_window(h)
            g = sdq[half, :, win]
            w = probs[half * 8 + h]
            p = w.astype(F32)
            gw = nt(g, keep(mask, sv[half, :, win]))
            pg = p * (gw * SCALE)
            gs = (pg - p * jnp.sum(pg, axis=-1, keepdims=True)).astype(BF)
            gq[:, win] += nn(gs, keep(mask, sk[half, :, win]))
            gk[:, win] += tn(gs, keep(mask, sq[half, :, win]))
            gv[:, win] += tn(w, keep(mask, g))
            return carry

        lax.fori_loop(0, 8, body, 0, unroll=4)

    def key_back(half):
        return remote(
            gsib_out.at[half], gsib_in.at[half], gs_s.at[half], gs_r.at[half], sib_dev
        )

    lanes, rows = pl.ds(0, HALF), pl.ds(0, ROWS)
    for half, w in ((0, ws_own), (1, ws_oth)):
        back_lanes(half, w, r_g[...].reshape(ROWS, D))
        spatial_back(half)
        gsib_out[half, 0] = gk[pl.ds(ROWS, ROWS), :].astype(BF)
        gsib_out[half, 1] = gv[pl.ds(ROWS, ROWS), :].astype(BF)
        key_back(half).start()
        if half == 0:
            sq[0] = gq[...].astype(BF)
            sk[0, rows] = gk[rows, :].astype(BF)
            sv[0, rows] = gv[rows, :].astype(BF)
    total = nn(sq[0, :, lanes], weight(ws_own, 0)) + nn(gq[:, lanes].astype(BF), weight(ws_oth, 0))
    key_back(0).wait()
    key = sk[0, rows, lanes].astype(F32) + gsib_in[0, 0, :, lanes].astype(F32)
    value = sv[0, rows, lanes].astype(F32) + gsib_in[0, 1, :, lanes].astype(F32)
    gh[...] = (
        total + nn(key.astype(BF), weight(ws_own, 1)) + nn(value.astype(BF), weight(ws_own, 2))
    )
    key_back(1).wait()

    def to_owner(n):
        piece = pl.ds(n * (ROWS // 2), ROWS // 2)
        return remote(v_out.at[piece], v_in.at[piece], end_s.at[n], end_r.at[n], swap_dev)

    for n in range(2):
        piece = pl.ds(n * (ROWS // 2), ROWS // 2)
        key = gk[piece, lanes] + gsib_in[1, 0, piece, lanes].astype(F32)
        value = gv[piece, lanes] + gsib_in[1, 1, piece, lanes].astype(F32)
        total = gh[piece, :] + nn(key.astype(BF), weight(ws_oth, 1))
        total += nn(value.astype(BF), weight(ws_oth, 2))
        normed, inverse = norm_stats(x_lat[piece, :].astype(F32))
        g_one = r_g[pl.ds(n * (GROUP // 2), GROUP // 2)].reshape(ROWS // 2, D).astype(F32)
        v_out[piece, :] = (norm_back(normed, inverse, total) + g_one).astype(BF)

        @pl.when(jnp.logical_not(stay))
        def _(n=n):
            to_owner(n).start()

    @pl.when(jnp.logical_not(stay))
    def _():
        remote(tr_out, tr_in, end_s.at[2], end_r.at[2], swap_dev).start()

    @pl.when(stay)
    def _():
        v_in[...] = v_out[...]
        tr_in[...] = tr_out[...]

    received(4, r_u)
    o_reached[...] = r_u[...].reshape(ROWS, D)
    received(5, r_d)
    extra = mean(own_prb[...].astype(F32) * r_d[...].reshape(ROWS, D).astype(F32))
    for n, ref, selfless in (
        (0, m_inner, stay), (1, m_adj, None), (2, m_tan, stay),
        (3, m_g, stay), (4, m_u, None), (5, m_d, None),
    ):
        sent(n, ref, selfless)

    @pl.when(jnp.logical_not(stay))
    def _():
        to_owner(0).wait()
        to_owner(1).wait()
        remote(tr_out, tr_in, end_s.at[2], end_r.at[2], swap_dev).wait()

    o_trace[...] = jnp.transpose(tr_in[...] + extra)[0:8]
    o_grads[...] = v_in[...]


def local(latent, probe, adjoint, spatial_qkv, spatial_proj, temporal_qkv, temporal_proj):
    def qkv(w):
        return jnp.transpose(w, (1, 2, 0)).reshape(3, 4, 144, D)

    def proj(w):
        return w.reshape(4, 144, D)

    dma = pltpu.SemaphoreType.DMA
    rows = pltpu.VMEM((ROWS, D), BF)
    weights = pltpu.VMEM((4, 4, 144, D), BF)
    one = pltpu.VMEM((2, ROWS, PAD), BF)
    two = pltpu.VMEM((2, 2 * ROWS, PAD), BF)
    message = pltpu.VMEM((GROUP, SPAN, D), BF)
    scratch = (
        [weights] * 4
        + [rows] * 5
        + [pltpu.VMEM((2, ROWS, D), BF)]
        + [one, two, two, one, two, two]
        + [pltpu.VMEM((16, ROWS, 2 * ROWS), BF)]
        + [one] * 3
        + [pltpu.VMEM((16, ROWS, ROWS), BF)]
        + [pltpu.VMEM((2, ROWS, PAD), F32)] * 2
        + [pltpu.VMEM((ROWS, PAD), F32)]
        + [pltpu.VMEM((2 * ROWS, PAD), F32)] * 2
        + [pltpu.VMEM((2, 2, ROWS, PAD), BF)] * 2
        + [pltpu.VMEM((ROWS, D), F32)]
        + [message] * 12
        + [rows] * 2
        + [pltpu.VMEM((ROWS, 128), F32)] * 2
        + [dma((3,)), dma((4,)), dma((2,)), dma((2,)), dma((2, 4)), dma((2, 4))]
        + [dma((2, 16)), dma((2, 16)), dma((2, 4)), dma((2, 4))]
        + [dma((6,)), dma((6,)), dma((2,)), dma((2,)), dma((3,)), dma((3,))]
        + [pltpu.SemaphoreType.REGULAR] * 2
    )
    reached, grads, trace = pl.pallas_call(
        kernel,
        out_shape=(
            jax.ShapeDtypeStruct((ROWS, D), BF),
            jax.ShapeDtypeStruct((ROWS, D), BF),
            jax.ShapeDtypeStruct((8, ROWS), F32),
        ),
        in_specs=[pl.BlockSpec(memory_space=pl.ANY)] * 7,
        out_specs=[pl.BlockSpec(memory_space=pltpu.VMEM)] * 3,
        scratch_shapes=scratch,
        compiler_params=pltpu.CompilerParams(
            collective_id=0, has_side_effects=True, vmem_limit_bytes=63 << 20
        ),
    )(
        latent, probe, adjoint,
        qkv(spatial_qkv), proj(spatial_proj), qkv(temporal_qkv), proj(temporal_proj),
    )
    new_latent = (0.5 * (latent.astype(F32) + reached[None].astype(F32))).astype(BF)
    new_adjoint = 1.5 * adjoint.astype(F32) - 0.5 * grads[None].astype(F32)
    return new_latent, new_adjoint, trace[0:1]


def solution(mesh):
    in_specs = (
        P("seq", "tp", None),
        P("seq", "tp", None),
        P("seq", "tp", None),
        P(None, None, "tp"),
        P("tp", None),
        P(None, None, "tp"),
        P("tp", None),
    )
    out_specs = (P("seq", "tp", None), P("seq", "tp", None), P("seq", "tp"))
    return jax.shard_map(local, mesh=mesh, in_specs=in_specs, out_specs=out_specs, check_vma=False)
```
